32 devices in a mesh: ctx: 4 (over x, core), tp: 8 (over z, y).
Axes of the slice: x: 2, y: 2, z: 4, core: 2. Of those that a mesh axis runs over, the one named last changes fastest.
Arguments:
- mamba_in: bfloat16 [4096, 16384], P(('ctx', 'tp')), may hold values from -6 to 6
- state_in_b: float32 [4096, 16], P('ctx'), may hold values from -6 to 6
- state_out_c: float32 [4096, 16], P('ctx'), may hold values from -1.5 to 1.5
- step_decay: float32 [4096, 256], P('ctx', 'tp'), may hold values from -1 to 0, as said below
- skip_gain: float32 [256], P('tp'), may hold values from 0.5 to 1.5
- queries: bfloat16 [4096, 8192], P(('ctx', 'tp')), may hold values from -6 to 6
- keys: bfloat16 [4096, 1024], P(('ctx', 'tp')), may hold values from -6 to 6
- values: bfloat16 [4096, 1024], P(('ctx', 'tp')), may hold values from -6 to 6
- doc_ids: int32 [32], replicated, may hold values from 0 to 3, never falling along the last dimension, each value on 1 to 20 neighbouring positions
Outputs:
- mamba_out: bfloat16 [4096, 16384], P(('ctx', 'tp'))
- attn_out: bfloat16 [4096, 8192], P(('ctx', 'tp'))
The draws below stay inside these ranges and needn't reach their ends.
Inputs may be any that keep to these rules, and one draw needn't show every extreme that they name: `step_decay`: strictly negative.
All inputs are finite; a program needn't handle non-finite values.
Results may differ from the reference program's by a relative error of at most 0.008.
Values may be sent and summed in bfloat16 or wider, within the bound.
A program may use at most 128 MiB of HBM per device.

```python
import math
import jax
import jax.numpy as jnp
import numpy as np
from jax import lax

DI = 16384
NS = 16
QH = 64
KVH = 8
HD = 128
P_SIZE = 64
SPAN = 128
BLK = 128
TOK_DEV = 1024
HM = 256
SEQUENCE_TOKENS = 4096
NBLK = 32
N_CTX = 4


def draw_queries(key, part):
    key = jax.random.fold_in(key, 101)
    base = jnp.clip(jax.random.normal(key, (SEQUENCE_TOKENS, QH * HD), jnp.float32), -6.0, 6.0)
    return base.astype(jnp.bfloat16)


def draw_keys(key, part):
    key = jax.random.fold_in(key, 202)
    base = jnp.clip(jax.random.normal(key, (SEQUENCE_TOKENS, KVH * HD), jnp.float32), -6.0, 6.0)
    return base.astype(jnp.bfloat16)


def draw_step_decay(key, part):
    key = jax.random.fold_in(key, 303)
    slow_share = 0.5
    is_slow = jax.random.uniform(jax.random.fold_in(key, 1), (HM,)) < slow_share
    fast_rate = jnp.exp(jax.random.uniform(jax.random.fold_in(key, 2), (HM,), jnp.float32, math.log(1.0 / 50.0), math.log(1.0 / 30.0)))
    slow_rate = jnp.exp(jax.random.uniform(jax.random.fold_in(key, 3), (HM,), jnp.float32, math.log(0.3), math.log(0.8))) / SEQUENCE_TOKENS
    decay_speed = jnp.where(is_slow, slow_rate, fast_rate)
    block_factor = jnp.exp(jax.random.uniform(jax.random.fold_in(key, 4), (NBLK, HM), jnp.float32, -math.log(2.0), math.log(2.0)))
    row_multiplier = jnp.repeat(block_factor, BLK, axis=0)
    approximate_estimate = jax.random.uniform(jax.random.fold_in(key, 5), (SEQUENCE_TOKENS, HM), jnp.float32, 0.5, 1.5)
    group_run_rows = jax.random.randint(jax.random.fold_in(key, 6), (3,), 0, SEQUENCE_TOKENS)
    group_run_length = jax.random.uniform(jax.random.fold_in(key, 7), (3,), jnp.float32, 0.22, 0.51)
    token_group_run = jnp.zeros((SEQUENCE_TOKENS,), jnp.float32).at[group_run_rows].set(group_run_length)
    return -(decay_speed[None, :] * row_multiplier * approximate_estimate) - token_group_run[:, None]


def block_levels(key, shape, split, low, largest):
    factor_of, own = 1.0, jax.random.fold_in(key, 6)
    for dim, shards_of in split:
        heights = jnp.exp(jax.random.uniform(jax.random.fold_in(own, dim), (shards_of,), jnp.float32, low / len(split), largest / len(split)))
        factor_of = factor_of * jnp.repeat(heights, shape[dim] // shards_of).reshape([-1 if axis == dim else 1 for axis in range(len(shape))])
    return factor_of


def split_up(amount, total, bound, slope):
    loads = [(1 << 20) // math.isqrt(grade ** slope) + 1 for grade in range(2, amount + 1)]
    surplus, given = total - bound - (amount - 1), [1] * (amount - 1)
    while surplus > 0:
        candidates = [i for i in range(amount - 1) if given[i] < bound]
        pool, remaining = sum([loads[i] for i in candidates]), surplus
        for i in candidates:
            addition = min(bound - given[i], max(1, remaining * loads[i] // pool), surplus)
            given[i] = given[i] + addition
            surplus = surplus - addition
    return np.array([bound] + given)


def ragged(rng, amount, total, reach, lean):
    if amount == 2:
        one = jax.random.randint(rng, (), max(1, total - reach), min(reach, total - 1) + 1)
        return jnp.stack([one, total - one])
    tallies = jnp.asarray(split_up(amount, total, reach, lean), jnp.int32)
    couples = (amount - 1) // 2
    donor, sink = tallies[1:1 + 2 * couples:2], tallies[2:2 + 2 * couples:2]
    margin = jnp.minimum(donor - 1, reach - sink)
    moved = jax.random.randint(jax.random.fold_in(rng, 1), (couples,), 0, 1 << 20) % (margin + 1)
    tallies = tallies.at[1:1 + 2 * couples:2].set(donor - moved).at[2:2 + 2 * couples:2].set(sink + moved)
    return tallies[jax.random.permutation(jax.random.fold_in(rng, 2), amount)]


def bell_draw(own_key, extent, scale, reach, shards=(), held_as=jnp.bfloat16):
    level = block_levels(own_key, extent, shards, -0.22, 0.18) if shards else 1.0
    values = jax.random.normal(own_key, extent, jnp.float32) * scale * level
    return jnp.minimum(jnp.maximum(values, -reach), reach).astype(held_as)


def setup_inputs(seed: int = 0) -> dict:
    streams_of = jax.random.split(jax.random.key(seed), 10)
    return {
        "mamba_in": bell_draw(streams_of[0], (SEQUENCE_TOKENS, DI), 1.0, 6.0, ((0, 32),)),
        "state_in_b": bell_draw(streams_of[1], (SEQUENCE_TOKENS, NS), 1.0, 6.0, ((0, 4),), jnp.float32),
        "state_out_c": bell_draw(streams_of[2], (SEQUENCE_TOKENS, NS), 0.25, 1.5, ((0, 4),), jnp.float32),
        "step_decay": draw_step_decay(jax.random.fold_in(streams_of[9], 71), 0),
        "skip_gain": jnp.clip(1.0 + 0.1 * jax.random.normal(streams_of[4], (HM,), jnp.float32), 0.5, 1.5),
        "queries": draw_queries(jax.random.fold_in(streams_of[9], 71), 0),
        "keys": draw_keys(jax.random.fold_in(streams_of[9], 71), 0),
        "values": bell_draw(streams_of[7], (SEQUENCE_TOKENS, KVH * HD), 1.0, 6.0, ((0, 32),)),
        "doc_ids": jnp.searchsorted(jnp.cumsum(ragged(streams_of[8], 4, NBLK, 5 * NBLK // 8, 0)), jnp.arange(NBLK), side="right").astype(jnp.int32),
    }


NEG_FILL = -1e+30
HIGHEST = lax.Precision.HIGHEST

def ssd_blocks(inputs, decay, state_in_b, state_out_c, initial, span_len):
    row_count, head_count, head_width = inputs.shape
    span_count = row_count // span_len
    inject = jnp.sqrt(-jnp.expm1(2.0 * decay))
    driven = (inputs * inject[:, :, None]).reshape(span_count, span_len, head_count, head_width)
    running = jnp.cumsum(decay.reshape(span_count, span_len, head_count), axis=1)
    b_blocks = state_in_b.reshape(span_count, span_len, -1)
    c_blocks = state_out_c.reshape(span_count, span_len, -1)
    causal_tri = jnp.tril(jnp.ones((span_len, span_len), dtype=bool))

    def advance(state_now, members):
        driven_c, running_c, b_span, c_span = members
        spread = running_c[:, None, :] - running_c[None, :, :]
        within = jnp.exp(jnp.where(causal_tri[:, :, None], spread, NEG_FILL))
        intersection = jnp.dot(c_span, b_span.T, precision=HIGHEST)
        inside = jnp.einsum('tsh,shp->thp', within * intersection[:, :, None], driven_c, precision=HIGHEST)
        entering = jnp.einsum('tn,hpn->thp', c_span, state_now, precision=HIGHEST) * jnp.exp(running_c)[:, :, None]
        remain = jnp.exp(running_c[-1][None, :] - running_c)
        state_next = state_now * jnp.exp(running_c[-1])[:, None, None] + jnp.einsum('shp,sn->hpn', driven_c * remain[:, :, None], b_span, precision=HIGHEST)
        return (state_next, inside + entering)
    final_state, outputs = lax.scan(advance, initial, (driven, running, b_blocks, c_blocks))
    return (outputs.reshape(row_count, head_count, head_width), final_state)

def reference(mamba_in, state_in_b, state_out_c, step_decay, skip_gain, queries, keys, values, doc_ids):
    inputs = mamba_in.astype(jnp.float32).reshape(SEQUENCE_TOKENS, HM, P_SIZE)
    initial = jnp.zeros((HM, P_SIZE, NS), jnp.float32)
    outputs, final_state = ssd_blocks(inputs, step_decay, state_in_b, state_out_c, initial, SPAN)
    mamba_out = (outputs + skip_gain[None, :, None] * inputs).reshape(SEQUENCE_TOKENS, DI).astype(jnp.bfloat16)
    score_scale = HD ** (-0.5)
    group_size = QH // KVH
    position = jnp.arange(SEQUENCE_TOKENS, dtype=jnp.int32)
    row_doc = doc_ids[position // BLK]
    query_groups = queries.reshape(SEQUENCE_TOKENS, KVH, group_size, HD)
    key_groups = keys.reshape(SEQUENCE_TOKENS, KVH, HD)
    value_groups = values.reshape(SEQUENCE_TOKENS, KVH, HD)
    pieces = []
    for block_index in range(N_CTX):
        low_row = block_index * TOK_DEV
        high_row = low_row + TOK_DEV
        visible = (row_doc[low_row:high_row, None] == row_doc[None, :high_row]) & (position[low_row:high_row, None] >= position[None, :high_row])

        def one_group(members):
            query_part, key_part, value_part = members
            scores = jnp.einsum('tgd,kd->gtk', query_part.astype(jnp.float32), key_part.astype(jnp.float32)) * score_scale
            scores = jnp.where(visible[None], scores, NEG_FILL)
            top_score = lax.optimization_barrier(jnp.max(scores, axis=-1, keepdims=True))
            terms = jnp.where(visible[None], jnp.exp(scores - top_score), 0.0)
            totals = lax.optimization_barrier(jnp.sum(terms, axis=-1))
            weights = terms.astype(jnp.bfloat16)
            context = jnp.einsum('gtk,kd->gtd', weights.astype(jnp.float32), value_part.astype(jnp.float32))
            return context / totals[:, :, None]
        result = lax.map(one_group, (jnp.transpose(query_groups[low_row:high_row], (1, 0, 2, 3)), jnp.transpose(key_groups[:high_row], (1, 0, 2)), jnp.transpose(value_groups[:high_row], (1, 0, 2))))
        pieces.append(jnp.transpose(result, (2, 0, 1, 3)).reshape(TOK_DEV, QH * HD))
    attn_out = jnp.concatenate(pieces, axis=0).astype(jnp.bfloat16)
    return (mamba_out, attn_out)
```

```python
import functools

import jax
import jax.numpy as jnp
from jax import lax
from jax.experimental import pallas as pl
from jax.experimental.pallas import tpu as pltpu
from jax.sharding import PartitionSpec as P

NS = 16
QH = 64
KVH = 8
HD = 128
P_SIZE = 64
BLK = 128
PAIR = 2 * P_SIZE
KEY_CHUNK = 512
LOG2E = 1.4426950408889634
NEG_FILL = -1e30
HIGHEST = lax.Precision.HIGHEST
F32 = jnp.float32
BF16 = jnp.bfloat16


def first_half(shape):
    return lax.broadcasted_iota(jnp.int32, shape, len(shape) - 1) < P_SIZE


def end_state_kernel(x_ref, weight_ref, bt_ref, out_ref):
    bt = bt_ref[...]
    low = first_half((NS, PAIR))
    for pair in range(x_ref.shape[1] // PAIR):
        cols = slice(pair * PAIR, (pair + 1) * PAIR)
        rows = [(bt * weight_ref[h : h + 1, :]).astype(BF16) for h in (2 * pair, 2 * pair + 1)]
        both = jnp.dot(
            jnp.concatenate(rows, axis=0), x_ref[:, cols], preferred_element_type=F32
        )
        out_ref[:, cols] = jnp.where(low, both[:NS], both[NS:]).astype(BF16)


def end_states(x, weight, bt, block):
    rows, channels = x.shape
    heads = block // P_SIZE
    return pl.pallas_call(
        end_state_kernel,
        grid=(channels // block,),
        in_specs=[
            pl.BlockSpec((rows, block), lambda i: (0, i)),
            pl.BlockSpec((heads, rows), lambda i: (i, 0)),
            pl.BlockSpec((NS, rows), lambda i: (0, 0)),
        ],
        out_specs=pl.BlockSpec((NS, block), lambda i: (0, i)),
        out_shape=jax.ShapeDtypeStruct((NS, channels), BF16),
        compiler_params=pltpu.CompilerParams(vmem_limit_bytes=24 << 20),
        cost_estimate=pl.CostEstimate(
            flops=4 * rows * NS * channels, bytes_accessed=2 * rows * channels, transcendentals=0
        ),
        name="end_states",
    )(x, weight, bt)


def prefix_kernel(spans, part_ref, total_ref, out_ref):
    state = jnp.zeros((NS, part_ref.shape[1]), F32)
    fade = jnp.exp(total_ref[...])
    for k in range(spans):
        rows = slice(k * NS, (k + 1) * NS)
        out_ref[rows, :] = state.astype(BF16)
        state = state * fade[k : k + 1, :] + part_ref[rows, :].astype(F32)


def prefix_states(parts, totals):
    return pl.pallas_call(
        functools.partial(prefix_kernel, totals.shape[0]),
        out_shape=jax.ShapeDtypeStruct(parts.shape, BF16),
        compiler_params=pltpu.CompilerParams(vmem_limit_bytes=16 << 20),
        cost_estimate=pl.CostEstimate(
            flops=2 * parts.size, bytes_accessed=4 * parts.size, transcendentals=totals.size
        ),
        name="prefix_states",
    )(parts, totals)


def span_kernel(x_ref, run_ref, runt_ref, cb_ref, c_ref, state_ref, gain_ref, out_ref):
    rows = x_ref.shape[0]
    meeting = cb_ref[...]
    c_rows = c_ref[...]
    low = first_half((rows, PAIR))
    low_row = jnp.where(first_half((1, PAIR)), 1.0, 0.0)
    keep_low = low_row.astype(BF16)
    keep_high = (1.0 - low_row).astype(BF16)
    for pair in range(x_ref.shape[1] // PAIR):
        cols = slice(pair * PAIR, (pair + 1) * PAIR)
        x_pair = x_ref[:, cols]
        mixers, fades = [], []
        for h in (2 * pair, 2 * pair + 1):
            run = run_ref[0, :, h : h + 1]
            spread = jnp.minimum(run - runt_ref[h : h + 1, :], 0.0)
            mixers.append((jnp.exp(spread) * meeting).astype(BF16))
            fades.append(jnp.exp(run))
        x_low, x_high = x_pair * keep_low, x_pair * keep_high
        if rows % 128 == 0:
            inside = jnp.dot(
                jnp.concatenate(mixers, axis=1),
                jnp.concatenate([x_low, x_high], axis=0),
                preferred_element_type=F32,
            )
        else:
            inside = jnp.dot(mixers[0], x_low, preferred_element_type=F32) + jnp.dot(
                mixers[1], x_high, preferred_element_type=F32
            )
        entering = jnp.dot(c_rows, state_ref[:, cols], preferred_element_type=F32)
        fade = jnp.where(low, fades[0], fades[1])
        out_ref[:, cols] = (
            inside + entering * fade + gain_ref[:, cols] * x_pair.astype(F32)
        ).astype(BF16)


def span_outputs(x, run, runt, meeting, c_rows, state, gain, block):
    rows, channels = x.shape
    heads = block // P_SIZE
    steps = channels // block
    run_blocks = run.reshape(rows, steps, heads).transpose(1, 0, 2)
    return pl.pallas_call(
        span_kernel,
        grid=(steps,),
        in_specs=[
            pl.BlockSpec((rows, block), lambda i: (0, i)),
            pl.BlockSpec((1, rows, heads), lambda i: (i, 0, 0)),
            pl.BlockSpec((heads, rows), lambda i: (i, 0)),
            pl.BlockSpec((rows, rows), lambda i: (0, 0)),
            pl.BlockSpec((rows, NS), lambda i: (0, 0)),
            pl.BlockSpec((NS, block), lambda i: (0, i)),
            pl.BlockSpec((1, block), lambda i: (0, i)),
        ],
        out_specs=pl.BlockSpec((rows, block), lambda i: (0, i)),
        out_shape=jax.ShapeDtypeStruct((rows, channels), BF16),
        compiler_params=pltpu.CompilerParams(vmem_limit_bytes=24 << 20),
        cost_estimate=pl.CostEstimate(
            flops=20 * rows * rows * channels,
            bytes_accessed=4 * rows * channels,
            transcendentals=rows * rows * channels // P_SIZE,
        ),
        name="span_outputs",
    )(x, run_blocks, runt, meeting, c_rows, state, gain)


def attention_kernel(heads, chunk, place_ref, lo_ref, q_ref, kv_ref, out_ref, vext, top, accum):
    step = pl.program_id(0)

    @pl.when(step == 0)
    def _():
        vext[:, :HD] = kv_ref[:, HD:]
        vext[:, HD:] = jnp.ones((vext.shape[0], HD), BF16)

    block = place_ref[0] + step
    lo_pos = lo_ref[step] * BLK
    last = (block * BLK) // chunk
    scale = HD ** (-0.5) * LOG2E

    def scores_of(head, start):
        q = q_ref[:, head * HD : (head + 1) * HD]
        k = kv_ref[pl.ds(start, chunk), :HD]
        return lax.dot_general(q, k, (((1,), (1,)), ((), ())), preferred_element_type=F32) * scale

    def gathered(terms, start):
        return jnp.dot(
            terms.astype(BF16), vext[pl.ds(start, chunk), :], preferred_element_type=F32
        )

    start = pl.multiple_of(last * chunk, chunk)
    key_pos = start + lax.broadcasted_iota(jnp.int32, (BLK, chunk), 1)
    query_pos = block * BLK + lax.broadcasted_iota(jnp.int32, (BLK, chunk), 0)
    visible = (key_pos <= query_pos) & (key_pos >= lo_pos)
    for head in range(heads):
        rows = slice(head * BLK, (head + 1) * BLK)
        scores = jnp.where(visible, scores_of(head, start), NEG_FILL)
        new_top = jnp.max(scores, axis=1, keepdims=True)
        top[rows, :] = jnp.broadcast_to(new_top, (BLK, HD))
        accum[rows, :] = gathered(jnp.exp2(scores - new_top), start)

    @pl.loop(lo_pos // chunk, last)
    def _(j):
        start = pl.multiple_of(j * chunk, chunk)
        key_pos = start + lax.broadcasted_iota(jnp.int32, (1, chunk), 1)
        hide = jnp.where(key_pos >= lo_pos, 0.0, NEG_FILL)
        for head in range(heads):
            rows = slice(head * BLK, (head + 1) * BLK)
            scores = scores_of(head, start) + hide
            old_top = top[rows, :]
            new_top = jnp.maximum(old_top, jnp.max(scores, axis=1, keepdims=True))
            top[rows, :] = new_top
            fade = jnp.exp2(old_top - new_top)
            added = gathered(jnp.exp2(scores - new_top[:, :1]), start)
            accum[rows, :HD] = accum[rows, :HD] * fade + added[:, :HD]
            accum[rows, HD:] = accum[rows, HD:] * fade + added[:, HD:]

    for head in range(heads):
        rows = slice(head * BLK, (head + 1) * BLK)
        out_ref[:, head * HD : (head + 1) * HD] = (
            accum[rows, :HD] / accum[rows, HD:]
        ).astype(BF16)


def attention(queries, kv, lo, place):
    rows, width = queries.shape
    heads = width // HD
    keys = kv.shape[0]
    chunk = min(KEY_CHUNK, keys)
    return pl.pallas_call(
        functools.partial(attention_kernel, heads, chunk),
        grid_spec=pltpu.PrefetchScalarGridSpec(
            num_scalar_prefetch=2,
            grid=(rows // BLK,),
            in_specs=[
                pl.BlockSpec((BLK, width), lambda i, *_: (i, 0)),
                pl.BlockSpec((keys, 2 * HD), lambda i, *_: (0, 0)),
            ],
            out_specs=pl.BlockSpec((BLK, width), lambda i, *_: (i, 0)),
            scratch_shapes=[
                pltpu.VMEM((keys, 2 * HD), BF16),
                pltpu.VMEM((heads * BLK, HD), F32),
                pltpu.VMEM((heads * BLK, 2 * HD), F32),
            ],
        ),
        out_shape=jax.ShapeDtypeStruct((rows, width), BF16),
        compiler_params=pltpu.CompilerParams(vmem_limit_bytes=32 << 20),
        cost_estimate=pl.CostEstimate(
            flops=4 * rows * width * keys // 2,
            bytes_accessed=4 * rows * width + 2 * kv.size,
            transcendentals=rows * heads * keys // 2,
        ),
        name="attention",
    )(place, lo, queries, kv)


def per_device(
    mamba_in, state_in_b, state_out_c, step_decay, skip_gain, queries, keys, values, doc_ids
):
    ctx_rank, tp_rank, tp = lax.axis_index("ctx"), lax.axis_index("tp"), lax.axis_size("tp")
    rows, channels = mamba_in.shape

    copies = tp // KVH
    kv_heads = jnp.concatenate(
        [keys.reshape(rows, KVH, HD), values.reshape(rows, KVH, HD)], axis=2
    )
    if copies > 1:
        kv_heads = jnp.repeat(kv_heads, copies, axis=1)
    kv_here = lax.all_to_all(
        kv_heads.reshape(rows, tp * 2 * HD), "tp", split_axis=1, concat_axis=0, tiled=True
    )
    query_cols = lax.all_to_all(queries, "tp", split_axis=1, concat_axis=0, tiled=True)
    kv = lax.all_gather(kv_here, "ctx", axis=0, tiled=True)

    decay = lax.all_to_all(step_decay, "tp", split_axis=0, concat_axis=1, tiled=True)
    gains = lax.all_gather(skip_gain, "tp", axis=0, tiled=True)
    b_rows = lax.dynamic_slice_in_dim(state_in_b, tp_rank * rows, rows, 0)
    c_rows = lax.dynamic_slice_in_dim(state_out_c, tp_rank * rows, rows, 0)
    lower = jnp.tril(jnp.ones((rows, rows), F32))
    decay_t = decay.T
    run = jnp.dot(lower, decay, precision=HIGHEST)
    run_t = jnp.dot(decay_t, lower.T, precision=HIGHEST)
    driven_run_t = run_t - 0.5 * jnp.log(-jnp.expm1(2.0 * decay_t))
    total = run_t[:, -1:]
    remain_t = jnp.exp(jnp.minimum(total - driven_run_t, 0.0))
    meeting = jnp.dot(c_rows, b_rows.T, precision=HIGHEST) * lower
    ends = end_states(mamba_in, remain_t, b_rows.T, 2048)
    everyone = ("ctx", "tp")
    parts = lax.all_to_all(ends, everyone, split_axis=1, concat_axis=0, tiled=True)
    total_row = jnp.repeat(total[:, 0], P_SIZE)[None, :]
    totals = lax.all_to_all(total_row, everyone, split_axis=1, concat_axis=0, tiled=True)
    before = prefix_states(parts, totals)
    state = lax.all_to_all(before, everyone, split_axis=0, concat_axis=1, tiled=True)

    lo_blocks = jnp.sum(doc_ids[None, :] < doc_ids[:, None], axis=1).astype(jnp.int32)
    blocks = query_cols.shape[0] // BLK
    place = ctx_rank * blocks
    lo = lax.dynamic_slice_in_dim(lo_blocks, place, blocks, 0)
    attn_rows = attention(query_cols, kv, lo, place.astype(jnp.int32)[None])

    attn_rows, state = lax.optimization_barrier((attn_rows, state))
    attn_out = lax.all_to_all(attn_rows, "tp", split_axis=0, concat_axis=1, tiled=True)
    mamba_out = span_outputs(
        mamba_in,
        run,
        driven_run_t,
        meeting,
        c_rows.astype(BF16),
        state,
        jnp.repeat(gains, P_SIZE)[None, :],
        1024,
    )
    return (mamba_out, attn_out)


def solution(mesh):
    in_specs = (
        P(("ctx", "tp"), None),
        P("ctx", None),
        P("ctx", None),
        P("ctx", "tp"),
        P("tp"),
        P(("ctx", "tp"), None),
        P(("ctx", "tp"), None),
        P(("ctx", "tp"), None),
        P(),
    )
    out_specs = (P(("ctx", "tp"), None), P(("ctx", "tp"), None))
    return jax.shard_map(
        per_device, mesh=mesh, in_specs=in_specs, out_specs=out_specs, check_vma=False
    )
```

```python
import functools

import jax
import jax.numpy as jnp
from jax import lax
from jax.experimental import pallas as pl
from jax.experimental.pallas import tpu as pltpu
from jax.sharding import PartitionSpec as P

NS = 16
QH = 64
KVH = 8
HD = 128
P_SIZE = 64
BLK = 128
PAIR = 2 * P_SIZE
KEY_CHUNK = 512
LOG2E = 1.4426950408889634
NEG_FILL = -1e30
HIGHEST = lax.Precision.HIGHEST
F32 = jnp.float32
BF16 = jnp.bfloat16


def first_half(shape):
    return lax.broadcasted_iota(jnp.int32, shape, len(shape) - 1) < P_SIZE


def end_state_kernel(x_ref, weight_ref, bt_ref, out_ref):
    bt = bt_ref[...]
    low = first_half((NS, PAIR))
    for pair in range(x_ref.shape[1] // PAIR):
        cols = slice(pair * PAIR, (pair + 1) * PAIR)
        rows = [(bt * weight_ref[h : h + 1, :]).astype(BF16) for h in (2 * pair, 2 * pair + 1)]
        both = jnp.dot(
            jnp.concatenate(rows, axis=0), x_ref[:, cols], preferred_element_type=F32
        )
        out_ref[:, cols] = jnp.where(low, both[:NS], both[NS:]).astype(BF16)


def end_states(x, weight, bt, block):
    rows, channels = x.shape
    heads = block // P_SIZE
    return pl.pallas_call(
        end_state_kernel,
        grid=(channels // block,),
        in_specs=[
            pl.BlockSpec((rows, block), lambda i: (0, i)),
            pl.BlockSpec((heads, rows), lambda i: (i, 0)),
            pl.BlockSpec((NS, rows), lambda i: (0, 0)),
        ],
        out_specs=pl.BlockSpec((NS, block), lambda i: (0, i)),
        out_shape=jax.ShapeDtypeStruct((NS, channels), BF16),
        compiler_params=pltpu.CompilerParams(vmem_limit_bytes=24 << 20),
        cost_estimate=pl.CostEstimate(
            flops=4 * rows * NS * channels, bytes_accessed=2 * rows * channels, transcendentals=0
        ),
        name="end_states",
    )(x, weight, bt)


def prefix_kernel(spans, part_ref, total_ref, out_ref):
    state = jnp.zeros((NS, part_ref.shape[1]), F32)
    fade = jnp.exp(total_ref[...])
    for k in range(spans):
        rows = slice(k * NS, (k + 1) * NS)
        out_ref[rows, :] = state.astype(BF16)
        state = state * fade[k : k + 1, :] + part_ref[rows, :].astype(F32)


def prefix_states(parts, totals):
    return pl.pallas_call(
        functools.partial(prefix_kernel, totals.shape[0]),
        out_shape=jax.ShapeDtypeStruct(parts.shape, BF16),
        compiler_params=pltpu.CompilerParams(vmem_limit_bytes=16 << 20),
        cost_estimate=pl.CostEstimate(
            flops=2 * parts.size, bytes_accessed=4 * parts.size, transcendentals=totals.size
        ),
        name="prefix_states",
    )(parts, totals)


def span_kernel(x_ref, run_ref, runt_ref, cb_ref, c_ref, state_ref, gain_ref, out_ref):
    rows = x_ref.shape[0]
    meeting = cb_ref[...]
    c_rows = c_ref[...]
    low = first_half((rows, PAIR))
    low_row = jnp.where(first_half((1, PAIR)), 1.0, 0.0)
    keep_low = low_row.astype(BF16)
    keep_high = (1.0 - low_row).astype(BF16)
    for pair in range(x_ref.shape[1] // PAIR):
        cols = slice(pair * PAIR, (pair + 1) * PAIR)
        x_pair = x_ref[:, cols]
        mixers, fades = [], []
        for h in (2 * pair, 2 * pair + 1):
            run = run_ref[0, :, h : h + 1]
            spread = jnp.minimum(run - runt_ref[h : h + 1, :], 0.0)
            mixers.append((jnp.exp(spread) * meeting).astype(BF16))
            fades.append(jnp.exp(run))
        x_low, x_high = x_pair * keep_low, x_pair * keep_high
        if rows % 128 == 0:
            inside = jnp.dot(
                jnp.concatenate(mixers, axis=1),
                jnp.concatenate([x_low, x_high], axis=0),
                preferred_element_type=F32,
            )
        else:
            inside = jnp.dot(mixers[0], x_low, preferred_element_type=F32) + jnp.dot(
                mixers[1], x_high, preferred_element_type=F32
            )
        entering = jnp.dot(c_rows, state_ref[:, cols], preferred_element_type=F32)
        fade = jnp.where(low, fades[0], fades[1])
        out_ref[:, cols] = (
            inside + entering * fade + gain_ref[:, cols] * x_pair.astype(F32)
        ).astype(BF16)


def span_outputs(x, run, runt, meeting, c_rows, state, gain, block):
    rows, channels = x.shape
    heads = block // P_SIZE
    steps = channels // block
    run_blocks = run.reshape(rows, steps, heads).transpose(1, 0, 2)
    return pl.pallas_call(
        span_kernel,
        grid=(steps,),
        in_specs=[
            pl.BlockSpec((rows, block), lambda i: (0, i)),
            pl.BlockSpec((1, rows, heads), lambda i: (i, 0, 0)),
            pl.BlockSpec((heads, rows), lambda i: (i, 0)),
            pl.BlockSpec((rows, rows), lambda i: (0, 0)),
            pl.BlockSpec((rows, NS), lambda i: (0, 0)),
            pl.BlockSpec((NS, block), lambda i: (0, i)),
            pl.BlockSpec((1, block), lambda i: (0, i)),
        ],
        out_specs=pl.BlockSpec((rows, block), lambda i: (0, i)),
        out_shape=jax.ShapeDtypeStruct((rows, channels), BF16),
        compiler_params=pltpu.CompilerParams(vmem_limit_bytes=24 << 20),
        cost_estimate=pl.CostEstimate(
            flops=20 * rows * rows * channels,
            bytes_accessed=4 * rows * channels,
            transcendentals=rows * rows * channels // P_SIZE,
        ),
        name="span_outputs",
    )(x, run_blocks, runt, meeting, c_rows, state, gain)


def attention_kernel(
    heads, chunk, first, spread, place_ref, lo_ref, q_ref, kv_ref, *refs
):
    out_ref, kext, vext, top, accum = refs[-5:]
    step = pl.program_id(0)
    rows_here = q_ref.shape[0]
    layers, ctxs, piece = spread
    keys = kext.shape[0]

    @pl.when(step == 0)
    def _():
        vext[:, HD:] = jnp.ones((keys, HD), BF16)
        for z in range(layers):
            for c in range(ctxs):
                src = slice((z * ctxs + c) * piece, (z * ctxs + c + 1) * piece)
                dst = slice((c * layers + z) * piece, (c * layers + z + 1) * piece)
                kext[dst, :] = kv_ref[src, :HD]
                vext[dst, :HD] = kv_ref[src, HD:]

    pos = place_ref[first + step]
    lo_pos = lo_ref[first + step]
    last = pos // chunk
    lo_chunk = lo_pos // chunk
    scale = HD ** (-0.5) * LOG2E
    together = min(heads, 4)
    tall = together * rows_here

    def scores_of(part, start):
        q = jnp.concatenate(
            [q_ref[:, h * HD : (h + 1) * HD] for h in range(part * together, (part + 1) * together)],
            axis=0,
        )
        k = kext[pl.ds(start, chunk), :]
        return lax.dot_general(q, k, (((1,), (1,)), ((), ())), preferred_element_type=F32) * scale

    def gathered(terms, start):
        return jnp.dot(
            terms.astype(BF16), vext[pl.ds(start, chunk), :], preferred_element_type=F32
        )

    start = pl.multiple_of(last * chunk, chunk)
    key_pos = start + lax.broadcasted_iota(jnp.int32, (rows_here, chunk), 1)
    query_pos = pos + lax.broadcasted_iota(jnp.int32, (rows_here, chunk), 0)
    bias = jnp.where((key_pos <= query_pos) & (key_pos >= lo_pos), 0.0, NEG_FILL)
    bias = jnp.concatenate([bias] * together, axis=0)
    for part in range(heads // together):
        rows = slice(part * tall, (part + 1) * tall)
        scores = scores_of(part, start) + bias
        new_top = jnp.max(scores, axis=1, keepdims=True)
        top[rows, :] = jnp.broadcast_to(new_top, (tall, HD))
        accum[rows, :] = gathered(jnp.exp2(scores - new_top), start)

    def more(j, hide):
        start = pl.multiple_of(j * chunk, chunk)
        for part in range(heads // together):
            rows = slice(part * tall, (part + 1) * tall)
            scores = scores_of(part, start)
            if hide is not None:
                scores = scores + hide
            old_top = top[rows, :]
            new_top = jnp.maximum(old_top, jnp.max(scores, axis=1, keepdims=True))
            top[rows, :] = new_top
            fade = jnp.exp2(old_top - new_top)
            added = gathered(jnp.exp2(scores - new_top[:, :1]), start)
            accum[rows, :HD] = accum[rows, :HD] * fade + added[:, :HD]
            accum[rows, HD:] = accum[rows, HD:] * fade + added[:, HD:]

    @pl.when(lo_chunk < last)
    def _():
        key_pos = lo_chunk * chunk + lax.broadcasted_iota(jnp.int32, (1, chunk), 1)
        more(lo_chunk, jnp.where(key_pos >= lo_pos, 0.0, NEG_FILL))

    @pl.loop(lo_chunk + 1, last)
    def _(j):
        more(j, None)

    for head in range(heads):
        rows = slice(head * rows_here, (head + 1) * rows_here)
        out_ref[:, head * HD : (head + 1) * HD] = (
            accum[rows, :HD] / accum[rows, HD:]
        ).astype(BF16)


def attention(queries, kv, place, lo, rows, spread, first, count, earlier=None):
    total, width = queries.shape
    heads = width // HD
    keys = kv.shape[0]
    chunk = min(KEY_CHUNK, keys)
    in_specs = [
        pl.BlockSpec((rows, width), lambda i, *_: (i + first, 0)),
        pl.BlockSpec((keys, 2 * HD), lambda i, *_: (0, 0)),
    ]
    operands = [place, lo, queries, kv]
    aliases = {}
    if earlier is not None:
        in_specs.append(pl.BlockSpec(memory_space=pl.ANY))
        operands.append(earlier)
        aliases = {4: 0}
    return pl.pallas_call(
        functools.partial(attention_kernel, heads, chunk, first, spread),
        grid_spec=pltpu.PrefetchScalarGridSpec(
            num_scalar_prefetch=2,
            grid=(count,),
            in_specs=in_specs,
            out_specs=pl.BlockSpec((rows, width), lambda i, *_: (i + first, 0)),
            scratch_shapes=[
                pltpu.VMEM((keys, HD), BF16),
                pltpu.VMEM((keys, 2 * HD), BF16),
                pltpu.VMEM((heads * rows, HD), F32),
                pltpu.VMEM((heads * rows, 2 * HD), F32),
            ],
        ),
        out_shape=jax.ShapeDtypeStruct((total, width), BF16),
        input_output_aliases=aliases,
        compiler_params=pltpu.CompilerParams(vmem_limit_bytes=40 << 20),
        cost_estimate=pl.CostEstimate(
            flops=4 * count * rows * width * keys // 2,
            bytes_accessed=4 * count * rows * width + 2 * kv.size,
            transcendentals=count * rows * heads * keys // 2,
        ),
        name="attention",
    )(*operands)


def per_device(
    mamba_in, state_in_b, state_out_c, step_decay, skip_gain, queries, keys, values, doc_ids
):
    tp_axes, plane, everyone = ("tz", "ty"), ("ctx", "ty"), ("ctx", "tz", "ty")
    layers, pairs, ctxs = lax.axis_size("tz"), lax.axis_size("ty"), lax.axis_size("ctx")
    tp, members = layers * pairs, ctxs * pairs
    layer = lax.axis_index("tz")
    tp_rank = layer * pairs + lax.axis_index("ty")
    rows, channels = mamba_in.shape
    groups = step_decay.shape[1]

    by_owner = step_decay.reshape(tp, rows, groups).transpose(0, 2, 1)
    gain_rows = jnp.pad(skip_gain[None, :], ((0, 7), (0, rows - groups)))
    sent = jnp.concatenate([by_owner, jnp.broadcast_to(gain_rows, (tp, 8, rows))], axis=1)
    got = lax.all_to_all(sent, tp_axes, split_axis=0, concat_axis=0, tiled=True)
    decay_t = got[:, :groups, :].reshape(tp * groups, rows)
    gains = got[:, groups, :groups].reshape(tp * groups)

    copies = members // KVH
    kv_heads = jnp.concatenate(
        [keys.reshape(rows, KVH, HD), values.reshape(rows, KVH, HD)], axis=2
    )
    if copies > 1:
        kv_heads = jnp.repeat(kv_heads, copies, axis=1)
    kv_here = lax.all_to_all(
        kv_heads.reshape(rows, members * 2 * HD), plane, split_axis=1, concat_axis=0, tiled=True
    )
    kv = lax.all_gather(kv_here, "tz", axis=0, tiled=True)
    query_cols = lax.all_to_all(queries, plane, split_axis=1, concat_axis=0, tiled=True)

    b_rows = lax.dynamic_slice_in_dim(state_in_b, tp_rank * rows, rows, 0)
    c_rows = lax.dynamic_slice_in_dim(state_out_c, tp_rank * rows, rows, 0)
    lower = jnp.tril(jnp.ones((rows, rows), F32))
    run_t = jnp.dot(decay_t, lower.T, precision=HIGHEST)
    run = run_t.T
    driven_run_t = run_t - 0.5 * jnp.log(-jnp.expm1(2.0 * decay_t))
    total = run_t[:, -1:]
    remain_t = jnp.exp(jnp.minimum(total - driven_run_t, 0.0))
    meeting = jnp.dot(c_rows, b_rows.T, precision=HIGHEST) * lower
    ends = end_states(mamba_in, remain_t, b_rows.T, 2048)
    total_row = jnp.repeat(total[:, 0], P_SIZE)[None, :]
    totals = lax.all_to_all(total_row, everyone, split_axis=1, concat_axis=0, tiled=True)

    member = jnp.arange(members, dtype=jnp.int32)
    place = ((member // pairs) * tp + layer * pairs + member % pairs) * rows
    docs_here = doc_ids[place // BLK]
    lo = BLK * jnp.sum(doc_ids[None, :] < docs_here[:, None], axis=1).astype(jnp.int32)
    spread = (layers, ctxs, pairs * rows)
    half = members // 2

    ends, query_cols = lax.optimization_barrier((ends, query_cols))
    parts = lax.all_to_all(ends, everyone, split_axis=1, concat_axis=0, tiled=True)
    attn_first = attention(query_cols, kv, place, lo, rows, spread, 0, half)
    parts, attn_first = lax.optimization_barrier((parts, attn_first))
    before = prefix_states(parts, totals)
    before, attn_first = lax.optimization_barrier((before, attn_first))
    state = lax.all_to_all(before, everyone, split_axis=0, concat_axis=1, tiled=True)
    attn_rows = attention(
        query_cols, kv, place, lo, rows, spread, half, members - half, attn_first
    )
    attn_rows, state = lax.optimization_barrier((attn_rows, state))
    attn_out = lax.all_to_all(attn_rows, plane, split_axis=0, concat_axis=1, tiled=True)
    mamba_out = span_outputs(
        mamba_in,
        run,
        driven_run_t,
        meeting,
        c_rows.astype(BF16),
        state,
        jnp.repeat(gains, P_SIZE)[None, :],
        1024,
    )
    return (mamba_out, attn_out)


def solution(mesh):
    ctxs, tp = mesh.devices.shape
    split = jax.sharding.Mesh(mesh.devices.reshape(ctxs, tp // 2, 2), ("ctx", "tz", "ty"))
    tokens = P(("ctx", "tz", "ty"), None)
    in_specs = (
        tokens,
        P("ctx", None),
        P("ctx", None),
        P("ctx", ("tz", "ty")),
        P(("tz", "ty")),
        tokens,
        tokens,
        tokens,
        P(),
    )
    return jax.shard_map(
        per_device, mesh=split, in_specs=in_specs, out_specs=(tokens, tokens), check_vma=False
    )
```

```python
import functools

import jax
import jax.numpy as jnp
from jax import lax
from jax.experimental import pallas as pl
from jax.experimental.pallas import tpu as pltpu
from jax.sharding import PartitionSpec as P

NS = 16
QH = 64
KVH = 8
HD = 128
P_SIZE = 64
BLK = 128
PAIR = 2 * P_SIZE
KEY_CHUNK = 512
LOG2E = 1.4426950408889634
NEG_FILL = -1e30
HIGHEST = lax.Precision.HIGHEST
F32 = jnp.float32
BF16 = jnp.bfloat16


def first_half(shape):
    return lax.broadcasted_iota(jnp.int32, shape, len(shape) - 1) < P_SIZE


def end_state_kernel(x_ref, weight_ref, bt_ref, out_ref):
    bt = bt_ref[...]
    low = first_half((NS, PAIR))
    for pair in range(x_ref.shape[1] // PAIR):
        cols = slice(pair * PAIR, (pair + 1) * PAIR)
        rows = [(bt * weight_ref[h : h + 1, :]).astype(BF16) for h in (2 * pair, 2 * pair + 1)]
        both = jnp.dot(
            jnp.concatenate(rows, axis=0), x_ref[:, cols], preferred_element_type=F32
        )
        out_ref[:, cols] = jnp.where(low, both[:NS], both[NS:]).astype(BF16)


def end_states(x, weight, bt, block):
    rows, channels = x.shape
    heads = block // P_SIZE
    return pl.pallas_call(
        end_state_kernel,
        grid=(channels // block,),
        in_specs=[
            pl.BlockSpec((rows, block), lambda i: (0, i)),
            pl.BlockSpec((heads, rows), lambda i: (i, 0)),
            pl.BlockSpec((NS, rows), lambda i: (0, 0)),
        ],
        out_specs=pl.BlockSpec((NS, block), lambda i: (0, i)),
        out_shape=jax.ShapeDtypeStruct((NS, channels), BF16),
        compiler_params=pltpu.CompilerParams(vmem_limit_bytes=24 << 20),
        cost_estimate=pl.CostEstimate(
            flops=4 * rows * NS * channels, bytes_accessed=2 * rows * channels, transcendentals=0
        ),
        name="end_states",
    )(x, weight, bt)


def prefix_kernel(spans, part_ref, total_ref, out_ref):
    state = jnp.zeros((NS, part_ref.shape[1]), F32)
    fade = jnp.exp(total_ref[...])
    for k in range(spans):
        rows = slice(k * NS, (k + 1) * NS)
        out_ref[rows, :] = state.astype(BF16)
        state = state * fade[k : k + 1, :] + part_ref[rows, :].astype(F32)


def prefix_states(parts, totals):
    return pl.pallas_call(
        functools.partial(prefix_kernel, totals.shape[0]),
        out_shape=jax.ShapeDtypeStruct(parts.shape, BF16),
        compiler_params=pltpu.CompilerParams(vmem_limit_bytes=16 << 20),
        cost_estimate=pl.CostEstimate(
            flops=2 * parts.size, bytes_accessed=4 * parts.size, transcendentals=totals.size
        ),
        name="prefix_states",
    )(parts, totals)


def span_kernel(x_ref, run_ref, runt_ref, cb_ref, c_ref, state_ref, gain_ref, out_ref):
    rows = x_ref.shape[0]
    meeting = cb_ref[...]
    c_rows = c_ref[...]
    low = first_half((rows, PAIR))
    low_row = jnp.where(first_half((1, PAIR)), 1.0, 0.0)
    keep_low = low_row.astype(BF16)
    keep_high = (1.0 - low_row).astype(BF16)
    for pair in range(x_ref.shape[1] // PAIR):
        cols = slice(pair * PAIR, (pair + 1) * PAIR)
        x_pair = x_ref[:, cols]
        mixers, fades = [], []
        for h in (2 * pair, 2 * pair + 1):
            run = run_ref[0, :, h : h + 1]
            spread = jnp.minimum(run - runt_ref[h : h + 1, :], 0.0)
            mixers.append((jnp.exp(spread) * meeting).astype(BF16))
            fades.append(jnp.exp(run))
        x_low, x_high = x_pair * keep_low, x_pair * keep_high
        if rows % 128 == 0:
            inside = jnp.dot(
                jnp.concatenate(mixers, axis=1),
                jnp.concatenate([x_low, x_high], axis=0),
                preferred_element_type=F32,
            )
        else:
            inside = jnp.dot(mixers[0], x_low, preferred_element_type=F32) + jnp.dot(
                mixers[1], x_high, preferred_element_type=F32
            )
        entering = jnp.dot(c_rows, state_ref[:, cols], preferred_element_type=F32)
        fade = jnp.where(low, fades[0], fades[1])
        out_ref[:, cols] = (
            inside + entering * fade + gain_ref[:, cols] * x_pair.astype(F32)
        ).astype(BF16)


def span_outputs(x, run, runt, meeting, c_rows, state, gain, block):
    rows, channels = x.shape
    heads = block // P_SIZE
    steps = channels // block
    run_blocks = run.reshape(rows, steps, heads).transpose(1, 0, 2)
    return pl.pallas_call(
        span_kernel,
        grid=(steps,),
        in_specs=[
            pl.BlockSpec((rows, block), lambda i: (0, i)),
            pl.BlockSpec((1, rows, heads), lambda i: (i, 0, 0)),
            pl.BlockSpec((heads, rows), lambda i: (i, 0)),
            pl.BlockSpec((rows, rows), lambda i: (0, 0)),
            pl.BlockSpec((rows, NS), lambda i: (0, 0)),
            pl.BlockSpec((NS, block), lambda i: (0, i)),
            pl.BlockSpec((1, block), lambda i: (0, i)),
        ],
        out_specs=pl.BlockSpec((rows, block), lambda i: (0, i)),
        out_shape=jax.ShapeDtypeStruct((rows, channels), BF16),
        compiler_params=pltpu.CompilerParams(vmem_limit_bytes=24 << 20),
        cost_estimate=pl.CostEstimate(
            flops=20 * rows * rows * channels,
            bytes_accessed=4 * rows * channels,
            transcendentals=rows * rows * channels // P_SIZE,
        ),
        name="span_outputs",
    )(x, run_blocks, runt, meeting, c_rows, state, gain)


def attention_kernel(
    heads, chunk, first, spread, place_ref, lo_ref, q_ref, kv_ref, *refs
):
    out_ref, kext, vext, top, accum = refs[-5:]
    step = pl.program_id(0)
    rows_here = q_ref.shape[0]
    layers, ctxs, piece = spread
    keys = kext.shape[0]

    @pl.when(step == 0)
    def _():
        vext[:, HD:] = jnp.ones((keys, HD), BF16)
        for z in range(layers):
            for c in range(ctxs):
                src = slice((z * ctxs + c) * piece, (z * ctxs + c + 1) * piece)
                dst = slice((c * layers + z) * piece, (c * layers + z + 1) * piece)
                kext[dst, :] = kv_ref[src, :HD]
                vext[dst, :HD] = kv_ref[src, HD:]

    pos = place_ref[first + step]
    lo_pos = lo_ref[first + step]
    last = pos // chunk
    lo_chunk = lo_pos // chunk
    scale = HD ** (-0.5) * LOG2E
    together = min(heads, 4)
    tall = together * rows_here

    def scores_of(part, start):
        q = jnp.concatenate(
            [q_ref[:, h * HD : (h + 1) * HD] for h in range(part * together, (part + 1) * together)],
            axis=0,
        )
        k = kext[pl.ds(start, chunk), :]
        return lax.dot_general(q, k, (((1,), (1,)), ((), ())), preferred_element_type=F32) * scale

    def gathered(terms, start):
        return jnp.dot(
            terms.astype(BF16), vext[pl.ds(start, chunk), :], preferred_element_type=F32
        )

    start = pl.multiple_of(last * chunk, chunk)
    key_pos = start + lax.broadcasted_iota(jnp.int32, (rows_here, chunk), 1)
    query_pos = pos + lax.broadcasted_iota(jnp.int32, (rows_here, chunk), 0)
    bias = jnp.where((key_pos <= query_pos) & (key_pos >= lo_pos), 0.0, NEG_FILL)
    bias = jnp.concatenate([bias] * together, axis=0)
    for part in range(heads // together):
        rows = slice(part * tall, (part + 1) * tall)
        scores = scores_of(part, start) + bias
        new_top = jnp.max(scores, axis=1, keepdims=True)
        top[rows, :] = jnp.broadcast_to(new_top, (tall, HD))
        accum[rows, :] = gathered(jnp.exp2(scores - new_top), start)

    def more(j, hide):
        start = pl.multiple_of(j * chunk, chunk)
        for part in range(heads // together):
            rows = slice(part * tall, (part + 1) * tall)
            scores = scores_of(part, start)
            if hide is not None:
                scores = scores + hide
            old_top = top[rows, :]
            new_top = jnp.maximum(old_top, jnp.max(scores, axis=1, keepdims=True))
            top[rows, :] = new_top
            fade = jnp.exp2(old_top - new_top)
            added = gathered(jnp.exp2(scores - new_top[:, :1]), start)
            accum[rows, :HD] = accum[rows, :HD] * fade + added[:, :HD]
            accum[rows, HD:] = accum[rows, HD:] * fade + added[:, HD:]

    @pl.when(lo_chunk < last)
    def _():
        key_pos = lo_chunk * chunk + lax.broadcasted_iota(jnp.int32, (1, chunk), 1)
        more(lo_chunk, jnp.where(key_pos >= lo_pos, 0.0, NEG_FILL))

    @pl.loop(lo_chunk + 1, last)
    def _(j):
        more(j, None)

    for head in range(heads):
        rows = slice(head * rows_here, (head + 1) * rows_here)
        out_ref[:, head * HD : (head + 1) * HD] = (
            accum[rows, :HD] / accum[rows, HD:]
        ).astype(BF16)


def attention(queries, kv, place, lo, rows, spread, first, count, earlier=None):
    total, width = queries.shape
    heads = width // HD
    keys = kv.shape[0]
    chunk = min(KEY_CHUNK, keys)
    in_specs = [
        pl.BlockSpec((rows, width), lambda i, *_: (i + first, 0)),
        pl.BlockSpec((keys, 2 * HD), lambda i, *_: (0, 0)),
    ]
    operands = [place, lo, queries, kv]
    aliases = {}
    if earlier is not None:
        in_specs.append(pl.BlockSpec(memory_space=pl.ANY))
        operands.append(earlier)
        aliases = {4: 0}
    return pl.pallas_call(
        functools.partial(attention_kernel, heads, chunk, first, spread),
        grid_spec=pltpu.PrefetchScalarGridSpec(
            num_scalar_prefetch=2,
            grid=(count,),
            in_specs=in_specs,
            out_specs=pl.BlockSpec((rows, width), lambda i, *_: (i + first, 0)),
            scratch_shapes=[
                pltpu.VMEM((keys, HD), BF16),
                pltpu.VMEM((keys, 2 * HD), BF16),
                pltpu.VMEM((heads * rows, HD), F32),
                pltpu.VMEM((heads * rows, 2 * HD), F32),
            ],
        ),
        out_shape=jax.ShapeDtypeStruct((total, width), BF16),
        input_output_aliases=aliases,
        compiler_params=pltpu.CompilerParams(vmem_limit_bytes=40 << 20),
        cost_estimate=pl.CostEstimate(
            flops=4 * count * rows * width * keys // 2,
            bytes_accessed=4 * count * rows * width + 2 * kv.size,
            transcendentals=count * rows * heads * keys // 2,
        ),
        name="attention",
    )(*operands)


def arrange_kernel(
    sizes, q_ref, k_ref, v_ref, d_ref, q_out, kv_out, d_out,
    own_sem, d_send, d_recv, k_send, k_recv, v_send, v_recv, q_send, q_recv,
    up_send, up_recv, down_send, down_recv,
):
    layers, ctxs, pairs, copies = sizes
    tp, members = layers * pairs, ctxs * pairs
    ctx, layer, pair = lax.axis_index("ctx"), lax.axis_index("tz"), lax.axis_index("ty")
    member, place = ctx * pairs + pair, layer * pairs + pair
    width = q_out.shape[2]

    def in_plane(j):
        return {"ctx": j // pairs, "ty": j % pairs}

    def in_tp(j):
        return {"tz": j // pairs, "ty": j % pairs}

    def send(src, dst, send_sem, recv_sem, device):
        return pltpu.make_async_remote_copy(
            src_ref=src,
            dst_ref=dst,
            send_sem=send_sem,
            recv_sem=recv_sem,
            device_id=device,
            device_id_type=pl.DeviceIdType.MESH,
        )

    def columns(j, size):
        return pl.ds(pl.multiple_of(j * size, size), size)

    barrier = pltpu.get_barrier_semaphore()
    for d in range(1, members):
        pl.semaphore_signal(
            barrier, inc=1, device_id=in_plane((member + d) % members),
            device_id_type=pl.DeviceIdType.MESH,
        )
    for d in range(1, tp):
        pl.semaphore_signal(
            barrier, inc=1, device_id=in_tp((place + d) % tp),
            device_id_type=pl.DeviceIdType.MESH,
        )
    pl.semaphore_wait(barrier, members - 1 + tp - 1)

    first, decays, later = [], [], []
    for d in range(1, members):
        j = (member + d) % members
        cols = columns(j // copies, HD)
        for src, half, s_sem, r_sem in (
            (k_ref, 0, k_send, k_recv),
            (v_ref, 1, v_send, v_recv),
        ):
            first.append(
                send(
                    src.at[:, cols],
                    kv_out.at[layer, member, :, half * HD : (half + 1) * HD],
                    s_sem.at[d - 1],
                    r_sem.at[d - 1],
                    in_plane(j),
                )
            )
    for copy in first:
        copy.start()
    for d in range(1, tp):
        j = (place + d) % tp
        decays.append(
            send(d_ref.at[j], d_out.at[place], d_send.at[d - 1], d_recv.at[d - 1], in_tp(j))
        )
    for copy in decays:
        copy.start()
    own_cols = columns(member // copies, HD)
    own_kv = [
        pltpu.make_async_copy(
            k_ref.at[:, own_cols], kv_out.at[layer, member, :, :HD], own_sem.at[0]
        ),
        pltpu.make_async_copy(
            v_ref.at[:, own_cols], kv_out.at[layer, member, :, HD:], own_sem.at[1]
        ),
    ]
    own_rest = [
        pltpu.make_async_copy(q_ref.at[:, columns(member, width)], q_out.at[member], own_sem.at[2]),
        pltpu.make_async_copy(d_ref.at[place], d_out.at[place], own_sem.at[3]),
    ]
    for copy in own_kv + own_rest:
        copy.start()
    for copy in own_kv:
        copy.wait()
    for copy in first:
        copy.wait_recv()

    def up(step, piece):
        block = kv_out.at[layer - step, piece * pairs : (piece + 1) * pairs]
        return send(
            block, block, up_send.at[step, piece], up_recv.at[step, piece], {"tz": layer + 1}
        )

    def down(step, piece):
        block = kv_out.at[layer + step, piece * pairs : (piece + 1) * pairs]
        return send(
            block, block, down_send.at[step, piece], down_recv.at[step, piece], {"tz": layer - 1}
        )

    for step in range(layers):
        for piece in range(ctxs):
            if step > 0:

                @pl.when(layer - step >= 0)
                def _():
                    up(step - 1, piece).wait_recv()

            if step < layers - 1:

                @pl.when((layer - step >= 0) & (layer < layers - 1))
                def _():
                    up(step, piece).start()

            if step > 0:

                @pl.when(layer + step <= layers - 1)
                def _():
                    down(step - 1, piece).wait_recv()

            if step < layers - 1:

                @pl.when((layer + step <= layers - 1) & (layer > 0))
                def _():
                    down(step, piece).start()

        if step == 0:
            for d in range(1, members):
                j = (member + d) % members
                later.append(
                    send(
                        q_ref.at[:, columns(j, width)],
                        q_out.at[member],
                        q_send.at[d - 1],
                        q_recv.at[d - 1],
                        in_plane(j),
                    )
                )
            for copy in later:
                copy.start()

    for step in range(layers - 1):
        for piece in range(ctxs):

            @pl.when((layer - step >= 0) & (layer < layers - 1))
            def _():
                up(step, piece).wait_send()

            @pl.when((layer + step <= layers - 1) & (layer > 0))
            def _():
                down(step, piece).wait_send()

    for copy in first:
        copy.wait_send()
    for copy in decays + later:
        copy.wait()
    for copy in own_rest:
        copy.wait()


def arrange(queries, keys, values, decays, sizes):
    layers, ctxs, pairs, _ = sizes
    tp, members = layers * pairs, ctxs * pairs
    rows = queries.shape[0]
    width = queries.shape[1] // members
    anywhere = pl.BlockSpec(memory_space=pl.ANY)
    dma = pltpu.SemaphoreType.DMA
    return pl.pallas_call(
        functools.partial(arrange_kernel, sizes),
        in_specs=[anywhere] * 4,
        out_specs=[anywhere] * 3,
        out_shape=[
            jax.ShapeDtypeStruct((members, rows, width), BF16),
            jax.ShapeDtypeStruct((layers, members, rows, 2 * HD), BF16),
            jax.ShapeDtypeStruct(decays.shape, F32),
        ],
        scratch_shapes=[dma((4,))]
        + [dma((tp - 1,))] * 2
        + [dma((members - 1,))] * 6
        + [dma((layers - 1, ctxs))] * 4,
        compiler_params=pltpu.CompilerParams(collective_id=0, has_side_effects=True),
        cost_estimate=pl.CostEstimate(
            flops=0, bytes_accessed=4 * queries.size, transcendentals=0
        ),
        name="arrange",
    )(queries, keys, values, decays)


def per_device(
    mamba_in, state_in_b, state_out_c, step_decay, skip_gain, queries, keys, values, doc_ids
):
    tp_axes, plane, everyone = ("tz", "ty"), ("ctx", "ty"), ("ctx", "tz", "ty")
    layers, pairs, ctxs = lax.axis_size("tz"), lax.axis_size("ty"), lax.axis_size("ctx")
    tp, members = layers * pairs, ctxs * pairs
    layer = lax.axis_index("tz")
    tp_rank = layer * pairs + lax.axis_index("ty")
    rows, channels = mamba_in.shape
    groups = step_decay.shape[1]

    by_owner = step_decay.reshape(tp, rows, groups).transpose(0, 2, 1)
    gain_rows = jnp.pad(skip_gain[None, :], ((0, 7), (0, rows - groups)))
    sent = jnp.concatenate([by_owner, jnp.broadcast_to(gain_rows, (tp, 8, rows))], axis=1)

    query_cols, kv, got = arrange(
        queries, keys, values, sent, (layers, ctxs, pairs, members // KVH)
    )
    query_cols = query_cols.reshape(members * rows, queries.shape[1] // members)
    kv = kv.reshape(layers * members * rows, 2 * HD)
    decay_t = got[:, :groups, :].reshape(tp * groups, rows)
    gains = got[:, groups, :groups].reshape(tp * groups)

    b_rows = lax.dynamic_slice_in_dim(state_in_b, tp_rank * rows, rows, 0)
    c_rows = lax.dynamic_slice_in_dim(state_out_c, tp_rank * rows, rows, 0)
    lower = jnp.tril(jnp.ones((rows, rows), F32))
    run_t = jnp.dot(decay_t, lower.T, precision=HIGHEST)
    run = run_t.T
    driven_run_t = run_t - 0.5 * jnp.log(-jnp.expm1(2.0 * decay_t))
    total = run_t[:, -1:]
    remain_t = jnp.exp(jnp.minimum(total - driven_run_t, 0.0))
    meeting = jnp.dot(c_rows, b_rows.T, precision=HIGHEST) * lower
    ends = end_states(mamba_in, remain_t, b_rows.T, 2048)
    span_sums = jnp.sum(step_decay.reshape(tp, rows, groups), axis=1)
    all_sums = lax.all_gather(span_sums, everyone).reshape(ctxs, tp, tp, groups)
    all_sums = all_sums.transpose(0, 2, 1, 3).reshape(ctxs * tp, tp * groups)
    heads_here = tp * groups // (ctxs * tp)
    flat = lax.axis_index("ctx") * tp + tp_rank
    sums_here = lax.dynamic_slice_in_dim(all_sums, flat * heads_here, heads_here, 1)
    totals = jnp.repeat(sums_here, P_SIZE, axis=1)

    member = jnp.arange(members, dtype=jnp.int32)
    place = ((member // pairs) * tp + layer * pairs + member % pairs) * rows
    docs_here = doc_ids[place // BLK]
    lo = BLK * jnp.sum(doc_ids[None, :] < docs_here[:, None], axis=1).astype(jnp.int32)
    spread = (layers, ctxs, pairs * rows)
    half = members // 2

    parts = lax.all_to_all(ends, everyone, split_axis=1, concat_axis=0, tiled=True)
    attn_first = attention(query_cols, kv, place, lo, rows, spread, 0, half)
    parts, attn_first = lax.optimization_barrier((parts, attn_first))
    before = prefix_states(parts, totals)
    before, attn_first = lax.optimization_barrier((before, attn_first))
    state = lax.all_to_all(before, everyone, split_axis=0, concat_axis=1, tiled=True)
    attn_rows = attention(
        query_cols, kv, place, lo, rows, spread, half, members - half, attn_first
    )
    attn_rows, state = lax.optimization_barrier((attn_rows, state))
    attn_out = lax.all_to_all(attn_rows, plane, split_axis=0, concat_axis=1, tiled=True)
    mamba_out = span_outputs(
        mamba_in,
        run,
        driven_run_t,
        meeting,
        c_rows.astype(BF16),
        state,
        jnp.repeat(gains, P_SIZE)[None, :],
        1024,
    )
    return (mamba_out, attn_out)


def solution(mesh):
    ctxs, tp = mesh.devices.shape
    split = jax.sharding.Mesh(mesh.devices.reshape(ctxs, tp // 2, 2), ("ctx", "tz", "ty"))
    tokens = P(("ctx", "tz", "ty"), None)
    in_specs = (
        tokens,
        P("ctx", None),
        P("ctx", None),
        P("ctx", ("tz", "ty")),
        P(("tz", "ty")),
        tokens,
        tokens,
        tokens,
        P(),
    )
    return jax.shard_map(
        per_device, mesh=split, in_specs=in_specs, out_specs=(tokens, tokens), check_vma=False
    )
```

```python
import functools

import jax
import jax.numpy as jnp
from jax import lax
from jax.experimental import pallas as pl
from jax.experimental.pallas import tpu as pltpu
from jax.sharding import PartitionSpec as P

NS = 16
QH = 64
KVH = 8
HD = 128
P_SIZE = 64
BLK = 128
PAIR = 2 * P_SIZE
KEY_CHUNK = 512
LOG2E = 1.4426950408889634
NEG_FILL = -1e30
HIGHEST = lax.Precision.HIGHEST
F32 = jnp.float32
BF16 = jnp.bfloat16


def first_half(shape):
    return lax.broadcasted_iota(jnp.int32, shape, len(shape) - 1) < P_SIZE


def end_state_kernel(x_ref, weight_ref, bt_ref, out_ref):
    bt = bt_ref[...]
    low = first_half((NS, PAIR))
    for pair in range(x_ref.shape[1] // PAIR):
        cols = slice(pair * PAIR, (pair + 1) * PAIR)
        rows = [(bt * weight_ref[h : h + 1, :]).astype(BF16) for h in (2 * pair, 2 * pair + 1)]
        both = jnp.dot(
            jnp.concatenate(rows, axis=0), x_ref[:, cols], preferred_element_type=F32
        )
        out_ref[:, cols] = jnp.where(low, both[:NS], both[NS:]).astype(BF16)


def end_states(x, weight, bt, block):
    rows, channels = x.shape
    heads = block // P_SIZE
    return pl.pallas_call(
        end_state_kernel,
        grid=(channels // block,),
        in_specs=[
            pl.BlockSpec((rows, block), lambda i: (0, i)),
            pl.BlockSpec((heads, rows), lambda i: (i, 0)),
            pl.BlockSpec((NS, rows), lambda i: (0, 0)),
        ],
        out_specs=pl.BlockSpec((NS, block), lambda i: (0, i)),
        out_shape=jax.ShapeDtypeStruct((NS, channels), BF16),
        compiler_params=pltpu.CompilerParams(vmem_limit_bytes=24 << 20),
        cost_estimate=pl.CostEstimate(
            flops=4 * rows * NS * channels, bytes_accessed=2 * rows * channels, transcendentals=0
        ),
        name="end_states",
    )(x, weight, bt)


def prefix_kernel(spans, part_ref, total_ref, out_ref):
    state = jnp.zeros((NS, part_ref.shape[1]), F32)
    fade = jnp.exp(total_ref[...])
    for k in range(spans):
        rows = slice(k * NS, (k + 1) * NS)
        out_ref[rows, :] = state.astype(BF16)
        state = state * fade[k : k + 1, :] + part_ref[rows, :].astype(F32)


def prefix_states(parts, totals):
    return pl.pallas_call(
        functools.partial(prefix_kernel, totals.shape[0]),
        out_shape=jax.ShapeDtypeStruct(parts.shape, BF16),
        compiler_params=pltpu.CompilerParams(vmem_limit_bytes=16 << 20),
        cost_estimate=pl.CostEstimate(
            flops=2 * parts.size, bytes_accessed=4 * parts.size, transcendentals=totals.size
        ),
        name="prefix_states",
    )(parts, totals)


def span_kernel(x_ref, run_ref, runt_ref, cb_ref, c_ref, state_ref, gain_ref, out_ref):
    rows = x_ref.shape[0]
    meeting = cb_ref[...]
    c_rows = c_ref[...]
    low = first_half((rows, PAIR))
    low_row = jnp.where(first_half((1, PAIR)), 1.0, 0.0)
    keep_low = low_row.astype(BF16)
    keep_high = (1.0 - low_row).astype(BF16)
    for pair in range(x_ref.shape[1] // PAIR):
        cols = slice(pair * PAIR, (pair + 1) * PAIR)
        x_pair = x_ref[:, cols]
        mixers, fades = [], []
        for h in (2 * pair, 2 * pair + 1):
            run = run_ref[0, :, h : h + 1]
            spread = jnp.minimum(run - runt_ref[h : h + 1, :], 0.0)
            mixers.append((jnp.exp(spread) * meeting).astype(BF16))
            fades.append(jnp.exp(run))
        x_low, x_high = x_pair * keep_low, x_pair * keep_high
        if rows % 128 == 0:
            inside = jnp.dot(
                jnp.concatenate(mixers, axis=1),
                jnp.concatenate([x_low, x_high], axis=0),
                preferred_element_type=F32,
            )
        else:
            inside = jnp.dot(mixers[0], x_low, preferred_element_type=F32) + jnp.dot(
                mixers[1], x_high, preferred_element_type=F32
            )
        entering = jnp.dot(c_rows, state_ref[:, cols], preferred_element_type=F32)
        fade = jnp.where(low, fades[0], fades[1])
        out_ref[:, cols] = (
            inside + entering * fade + gain_ref[:, cols] * x_pair.astype(F32)
        ).astype(BF16)


def span_outputs(x, run, runt, meeting, c_rows, state, gain, block):
    rows, channels = x.shape
    heads = block // P_SIZE
    steps = channels // block
    run_blocks = run.reshape(rows, steps, heads).transpose(1, 0, 2)
    return pl.pallas_call(
        span_kernel,
        grid=(steps,),
        in_specs=[
            pl.BlockSpec((rows, block), lambda i: (0, i)),
            pl.BlockSpec((1, rows, heads), lambda i: (i, 0, 0)),
            pl.BlockSpec((heads, rows), lambda i: (i, 0)),
            pl.BlockSpec((rows, rows), lambda i: (0, 0)),
            pl.BlockSpec((rows, NS), lambda i: (0, 0)),
            pl.BlockSpec((NS, block), lambda i: (0, i)),
            pl.BlockSpec((1, block), lambda i: (0, i)),
        ],
        out_specs=pl.BlockSpec((rows, block), lambda i: (0, i)),
        out_shape=jax.ShapeDtypeStruct((rows, channels), BF16),
        compiler_params=pltpu.CompilerParams(vmem_limit_bytes=24 << 20),
        cost_estimate=pl.CostEstimate(
            flops=20 * rows * rows * channels,
            bytes_accessed=4 * rows * channels,
            transcendentals=rows * rows * channels // P_SIZE,
        ),
        name="span_outputs",
    )(x, run_blocks, runt, meeting, c_rows, state, gain)


def attention_kernel(
    heads, chunk, first, spread, place_ref, lo_ref, q_ref, kv_ref, *refs
):
    out_ref, kext, vext, top, accum = refs[-5:]
    step = pl.program_id(0)
    rows_here = q_ref.shape[0]
    layers, ctxs, piece = spread
    keys = kext.shape[0]

    @pl.when(step == 0)
    def _():
        vext[:, HD:] = jnp.ones((keys, HD), BF16)
        for z in range(layers):
            for c in range(ctxs):
                src = slice((z * ctxs + c) * piece, (z * ctxs + c + 1) * piece)
                dst = slice((c * layers + z) * piece, (c * layers + z + 1) * piece)
                kext[dst, :] = kv_ref[src, :HD]
                vext[dst, :HD] = kv_ref[src, HD:]

    pos = place_ref[first + step]
    lo_pos = lo_ref[first + step]
    last = pos // chunk
    lo_chunk = lo_pos // chunk
    scale = HD ** (-0.5) * LOG2E
    together = min(heads, 4)
    tall = together * rows_here

    def scores_of(part, start):
        q = jnp.concatenate(
            [q_ref[:, h * HD : (h + 1) * HD] for h in range(part * together, (part + 1) * together)],
            axis=0,
        )
        k = kext[pl.ds(start, chunk), :]
        return lax.dot_general(q, k, (((1,), (1,)), ((), ())), preferred_element_type=F32) * scale

    def gathered(terms, start):
        return jnp.dot(
            terms.astype(BF16), vext[pl.ds(start, chunk), :], preferred_element_type=F32
        )

    start = pl.multiple_of(last * chunk, chunk)
    key_pos = start + lax.broadcasted_iota(jnp.int32, (rows_here, chunk), 1)
    query_pos = pos + lax.broadcasted_iota(jnp.int32, (rows_here, chunk), 0)
    bias = jnp.where((key_pos <= query_pos) & (key_pos >= lo_pos), 0.0, NEG_FILL)
    bias = jnp.concatenate([bias] * together, axis=0)
    for part in range(heads // together):
        rows = slice(part * tall, (part + 1) * tall)
        scores = scores_of(part, start) + bias
        new_top = jnp.max(scores, axis=1, keepdims=True)
        top[rows, :] = jnp.broadcast_to(new_top, (tall, HD))
        accum[rows, :] = gathered(jnp.exp2(scores - new_top), start)

    def more(j, hide):
        start = pl.multiple_of(j * chunk, chunk)
        for part in range(heads // together):
            rows = slice(part * tall, (part + 1) * tall)
            scores = scores_of(part, start)
            if hide is not None:
                scores = scores + hide
            old_top = top[rows, :]
            new_top = jnp.maximum(old_top, jnp.max(scores, axis=1, keepdims=True))
            top[rows, :] = new_top
            fade = jnp.exp2(old_top - new_top)
            added = gathered(jnp.exp2(scores - new_top[:, :1]), start)
            accum[rows, :HD] = accum[rows, :HD] * fade + added[:, :HD]
            accum[rows, HD:] = accum[rows, HD:] * fade + added[:, HD:]

    @pl.when(lo_chunk < last)
    def _():
        key_pos = lo_chunk * chunk + lax.broadcasted_iota(jnp.int32, (1, chunk), 1)
        more(lo_chunk, jnp.where(key_pos >= lo_pos, 0.0, NEG_FILL))

    @pl.loop(lo_chunk + 1, last)
    def _(j):
        more(j, None)

    for head in range(heads):
        rows = slice(head * rows_here, (head + 1) * rows_here)
        out_ref[:, head * HD : (head + 1) * HD] = (
            accum[rows, :HD] / accum[rows, HD:]
        ).astype(BF16)


def attention(queries, kv, place, lo, rows, spread, first, count, earlier=None):
    total, width = queries.shape
    heads = width // HD
    keys = kv.shape[0]
    chunk = min(KEY_CHUNK, keys)
    in_specs = [
        pl.BlockSpec((rows, width), lambda i, *_: (i + first, 0)),
        pl.BlockSpec((keys, 2 * HD), lambda i, *_: (0, 0)),
    ]
    operands = [place, lo, queries, kv]
    aliases = {}
    if earlier is not None:
        in_specs.append(pl.BlockSpec(memory_space=pl.ANY))
        operands.append(earlier)
        aliases = {4: 0}
    return pl.pallas_call(
        functools.partial(attention_kernel, heads, chunk, first, spread),
        grid_spec=pltpu.PrefetchScalarGridSpec(
            num_scalar_prefetch=2,
            grid=(count,),
            in_specs=in_specs,
            out_specs=pl.BlockSpec((rows, width), lambda i, *_: (i + first, 0)),
            scratch_shapes=[
                pltpu.VMEM((keys, HD), BF16),
                pltpu.VMEM((keys, 2 * HD), BF16),
                pltpu.VMEM((heads * rows, HD), F32),
                pltpu.VMEM((heads * rows, 2 * HD), F32),
            ],
        ),
        out_shape=jax.ShapeDtypeStruct((total, width), BF16),
        input_output_aliases=aliases,
        compiler_params=pltpu.CompilerParams(vmem_limit_bytes=40 << 20),
        cost_estimate=pl.CostEstimate(
            flops=4 * count * rows * width * keys // 2,
            bytes_accessed=4 * count * rows * width + 2 * kv.size,
            transcendentals=count * rows * heads * keys // 2,
        ),
        name="attention",
    )(*operands)


def arrange_kernel(
    sizes, q_ref, k_ref, v_ref, d_ref, q_out, kv_out, d_out,
    own_sem, d_send, d_recv, k_send, k_recv, v_send, v_recv, q_send, q_recv,
    up_send, up_recv, down_send, down_recv,
):
    layers, ctxs, pairs, copies = sizes
    tp, members = layers * pairs, ctxs * pairs
    ctx, layer, pair = lax.axis_index("ctx"), lax.axis_index("tz"), lax.axis_index("ty")
    member, place = ctx * pairs + pair, layer * pairs + pair
    width = q_out.shape[2]

    def in_plane(j):
        return {"ctx": j // pairs, "ty": j % pairs}

    def in_tp(j):
        return {"tz": j // pairs, "ty": j % pairs}

    def send(src, dst, send_sem, recv_sem, device):
        return pltpu.make_async_remote_copy(
            src_ref=src,
            dst_ref=dst,
            send_sem=send_sem,
            recv_sem=recv_sem,
            device_id=device,
            device_id_type=pl.DeviceIdType.MESH,
        )

    def columns(j, size):
        return pl.ds(pl.multiple_of(j * size, size), size)

    barrier = pltpu.get_barrier_semaphore()
    for d in range(1, members):
        pl.semaphore_signal(
            barrier, inc=1, device_id=in_plane((member + d) % members),
            device_id_type=pl.DeviceIdType.MESH,
        )
    for d in range(1, tp):
        pl.semaphore_signal(
            barrier, inc=1, device_id=in_tp((place + d) % tp),
            device_id_type=pl.DeviceIdType.MESH,
        )
    pl.semaphore_wait(barrier, members - 1 + tp - 1)

    first, decays, later = [], [], []
    for d in range(1, members):
        j = (member + d) % members
        cols = columns(j // copies, HD)
        for src, half, s_sem, r_sem in (
            (k_ref, 0, k_send, k_recv),
            (v_ref, 1, v_send, v_recv),
        ):
            first.append(
                send(
                    src.at[:, cols],
                    kv_out.at[layer, member, :, half * HD : (half + 1) * HD],
                    s_sem.at[d - 1],
                    r_sem.at[d - 1],
                    in_plane(j),
                )
            )
    for copy in first:
        copy.start()
    for d in range(1, tp):
        j = (place + d) % tp
        decays.append(
            send(d_ref.at[j], d_out.at[place], d_send.at[d - 1], d_recv.at[d - 1], in_tp(j))
        )
    for copy in decays:
        copy.start()
    own_cols = columns(member // copies, HD)
    own_kv = [
        pltpu.make_async_copy(
            k_ref.at[:, own_cols], kv_out.at[layer, member, :, :HD], own_sem.at[0]
        ),
        pltpu.make_async_copy(
            v_ref.at[:, own_cols], kv_out.at[layer, member, :, HD:], own_sem.at[1]
        ),
    ]
    own_rest = [
        pltpu.make_async_copy(q_ref.at[:, columns(member, width)], q_out.at[member], own_sem.at[2]),
        pltpu.make_async_copy(d_ref.at[place], d_out.at[place], own_sem.at[3]),
    ]
    for copy in own_kv + own_rest:
        copy.start()
    for copy in own_kv:
        copy.wait()
    for copy in first:
        copy.wait_recv()

    def up(step, piece):
        block = kv_out.at[layer - step, piece * pairs : (piece + 1) * pairs]
        return send(
            block, block, up_send.at[step, piece], up_recv.at[step, piece], {"tz": layer + 1}
        )

    def down(step, piece):
        block = kv_out.at[layer + step, piece * pairs : (piece + 1) * pairs]
        return send(
            block, block, down_send.at[step, piece], down_recv.at[step, piece], {"tz": layer - 1}
        )

    for step in range(layers):
        for piece in range(ctxs):
            if step > 0:

                @pl.when(layer - step >= 0)
                def _():
                    up(step - 1, piece).wait_recv()

            if step < layers - 1:

                @pl.when((layer - step >= 0) & (layer < layers - 1))
                def _():
                    up(step, piece).start()

            if step > 0:

                @pl.when(layer + step <= layers - 1)
                def _():
                    down(step - 1, piece).wait_recv()

            if step < layers - 1:

                @pl.when((layer + step <= layers - 1) & (layer > 0))
                def _():
                    down(step, piece).start()

        if step == 0:
            for d in range(1, members):
                j = (member + d) % members
                later.append(
                    send(
                        q_ref.at[:, columns(j, width)],
                        q_out.at[member],
                        q_send.at[d - 1],
                        q_recv.at[d - 1],
                        in_plane(j),
                    )
                )
            for copy in later:
                copy.start()

    for step in range(layers - 1):
        for piece in range(ctxs):

            @pl.when((layer - step >= 0) & (layer < layers - 1))
            def _():
                up(step, piece).wait_send()

            @pl.when((layer + step <= layers - 1) & (layer > 0))
            def _():
                down(step, piece).wait_send()

    for copy in first:
        copy.wait_send()
    for copy in decays + later:
        copy.wait()
    for copy in own_rest:
        copy.wait()


def arrange(queries, keys, values, decays, sizes):
    layers, ctxs, pairs, _ = sizes
    tp, members = layers * pairs, ctxs * pairs
    rows = queries.shape[0]
    width = queries.shape[1] // members
    anywhere = pl.BlockSpec(memory_space=pl.ANY)
    dma = pltpu.SemaphoreType.DMA
    return pl.pallas_call(
        functools.partial(arrange_kernel, sizes),
        in_specs=[anywhere] * 4,
        out_specs=[anywhere] * 3,
        out_shape=[
            jax.ShapeDtypeStruct((members, rows, width), BF16),
            jax.ShapeDtypeStruct((layers, members, rows, 2 * HD), BF16),
            jax.ShapeDtypeStruct(decays.shape, F32),
        ],
        scratch_shapes=[dma((4,))]
        + [dma((tp - 1,))] * 2
        + [dma((members - 1,))] * 6
        + [dma((layers - 1, ctxs))] * 4,
        compiler_params=pltpu.CompilerParams(collective_id=0, has_side_effects=True),
        cost_estimate=pl.CostEstimate(
            flops=0, bytes_accessed=4 * queries.size, transcendentals=0
        ),
        name="arrange",
    )(queries, keys, values, decays)


def per_device(
    mamba_in, state_in_b, state_out_c, step_decay, skip_gain, queries, keys, values, doc_ids
):
    tp_axes, plane, everyone = ("tz", "ty"), ("ctx", "ty"), ("ctx", "tz", "ty")
    layers, pairs, ctxs = lax.axis_size("tz"), lax.axis_size("ty"), lax.axis_size("ctx")
    tp, members = layers * pairs, ctxs * pairs
    layer = lax.axis_index("tz")
    tp_rank = layer * pairs + lax.axis_index("ty")
    rows, channels = mamba_in.shape
    groups = step_decay.shape[1]

    by_owner = step_decay.reshape(tp, rows, groups).transpose(0, 2, 1)
    gain_rows = jnp.pad(skip_gain[None, :], ((0, 7), (0, rows - groups)))
    sent = jnp.concatenate([by_owner, jnp.broadcast_to(gain_rows, (tp, 8, rows))], axis=1)

    query_cols, kv, got = arrange(
        queries, keys, values, sent, (layers, ctxs, pairs, members // KVH)
    )
    query_cols = query_cols.reshape(members * rows, queries.shape[1] // members)
    kv = kv.reshape(layers * members * rows, 2 * HD)
    decay_t = got[:, :groups, :].reshape(tp * groups, rows)
    gains = got[:, groups, :groups].reshape(tp * groups)

    b_rows = lax.dynamic_slice_in_dim(state_in_b, tp_rank * rows, rows, 0)
    c_rows = lax.dynamic_slice_in_dim(state_out_c, tp_rank * rows, rows, 0)
    lower = jnp.tril(jnp.ones((rows, rows), F32))
    run_t = jnp.dot(decay_t, lower.T, precision=HIGHEST)
    run = run_t.T
    driven_run_t = run_t - 0.5 * jnp.log(-jnp.expm1(2.0 * decay_t))
    total = run_t[:, -1:]
    remain_t = jnp.exp(jnp.minimum(total - driven_run_t, 0.0))
    meeting = jnp.dot(c_rows, b_rows.T, precision=HIGHEST) * lower
    ends = end_states(mamba_in, remain_t, b_rows.T, 2048)
    total_row = jnp.repeat(total[:, 0], P_SIZE)[None, :]
    totals = lax.all_to_all(total_row, everyone, split_axis=1, concat_axis=0, tiled=True)

    member = jnp.arange(members, dtype=jnp.int32)
    place = ((member // pairs) * tp + layer * pairs + member % pairs) * rows
    docs_here = doc_ids[place // BLK]
    lo = BLK * jnp.sum(doc_ids[None, :] < docs_here[:, None], axis=1).astype(jnp.int32)
    spread = (layers, ctxs, pairs * rows)
    half = members // 2

    parts = lax.all_to_all(ends, everyone, split_axis=1, concat_axis=0, tiled=True)
    attn_first = attention(query_cols, kv, place, lo, rows, spread, 0, half)
    parts, attn_first = lax.optimization_barrier((parts, attn_first))
    before = prefix_states(parts, totals)
    before, attn_first = lax.optimization_barrier((before, attn_first))
    state = lax.all_to_all(before, everyone, split_axis=0, concat_axis=1, tiled=True)
    attn_rows = attention(
        query_cols, kv, place, lo, rows, spread, half, members - half, attn_first
    )
    attn_rows, state = lax.optimization_barrier((attn_rows, state))
    attn_out = lax.all_to_all(attn_rows, plane, split_axis=0, concat_axis=1, tiled=True)
    mamba_out = span_outputs(
        mamba_in,
        run,
        driven_run_t,
        meeting,
        c_rows.astype(BF16),
        state,
        jnp.repeat(gains, P_SIZE)[None, :],
        1024,
    )
    return (mamba_out, attn_out)


def solution(mesh):
    ctxs, tp = mesh.devices.shape
    split = jax.sharding.Mesh(mesh.devices.reshape(ctxs, tp // 2, 2), ("ctx", "tz", "ty"))
    tokens = P(("ctx", "tz", "ty"), None)
    in_specs = (
        tokens,
        P("ctx", None),
        P("ctx", None),
        P("ctx", ("tz", "ty")),
        P(("tz", "ty")),
        tokens,
        tokens,
        tokens,
        P(),
    )
    return jax.shard_map(
        per_device, mesh=split, in_specs=in_specs, out_specs=(tokens, tokens), check_vma=False
    )
```

```python
import functools

import jax
import jax.numpy as jnp
from jax import lax
from jax.experimental import pallas as pl
from jax.experimental.pallas import tpu as pltpu
from jax.sharding import PartitionSpec as P

NS = 16
QH = 64
KVH = 8
HD = 128
P_SIZE = 64
BLK = 128
PAIR = 2 * P_SIZE
KEY_CHUNK = 256
LOG2E = 1.4426950408889634
NEG_FILL = -1e30
HIGHEST = lax.Precision.HIGHEST
F32 = jnp.float32
BF16 = jnp.bfloat16


def first_half(shape):
    return lax.broadcasted_iota(jnp.int32, shape, len(shape) - 1) < P_SIZE


def end_state_kernel(x_ref, weight_ref, bt_ref, out_ref):
    bt = bt_ref[...]
    low = first_half((NS, PAIR))
    for pair in range(x_ref.shape[1] // PAIR):
        cols = slice(pair * PAIR, (pair + 1) * PAIR)
        rows = [(bt * weight_ref[h : h + 1, :]).astype(BF16) for h in (2 * pair, 2 * pair + 1)]
        both = jnp.dot(
            jnp.concatenate(rows, axis=0), x_ref[:, cols], preferred_element_type=F32
        )
        out_ref[:, cols] = jnp.where(low, both[:NS], both[NS:]).astype(BF16)


def end_states(x, weight, bt, block):
    rows, channels = x.shape
    heads = block // P_SIZE
    return pl.pallas_call(
        end_state_kernel,
        grid=(channels // block,),
        in_specs=[
            pl.BlockSpec((rows, block), lambda i: (0, i)),
            pl.BlockSpec((heads, rows), lambda i: (i, 0)),
            pl.BlockSpec((NS, rows), lambda i: (0, 0)),
        ],
        out_specs=pl.BlockSpec((NS, block), lambda i: (0, i)),
        out_shape=jax.ShapeDtypeStruct((NS, channels), BF16),
        compiler_params=pltpu.CompilerParams(vmem_limit_bytes=24 << 20),
        cost_estimate=pl.CostEstimate(
            flops=4 * rows * NS * channels, bytes_accessed=2 * rows * channels, transcendentals=0
        ),
        name="end_states",
    )(x, weight, bt)


def prefix_kernel(spans, part_ref, total_ref, out_ref):
    state = jnp.zeros((NS, part_ref.shape[1]), F32)
    fade = jnp.exp(total_ref[...])
    for k in range(spans):
        rows = slice(k * NS, (k + 1) * NS)
        out_ref[rows, :] = state.astype(BF16)
        state = state * fade[k : k + 1, :] + part_ref[rows, :].astype(F32)


def prefix_states(parts, totals):
    return pl.pallas_call(
        functools.partial(prefix_kernel, totals.shape[0]),
        out_shape=jax.ShapeDtypeStruct(parts.shape, BF16),
        compiler_params=pltpu.CompilerParams(vmem_limit_bytes=16 << 20),
        cost_estimate=pl.CostEstimate(
            flops=2 * parts.size, bytes_accessed=4 * parts.size, transcendentals=totals.size
        ),
        name="prefix_states",
    )(parts, totals)


def span_kernel(x_ref, run_ref, runt_ref, cb_ref, c_ref, state_ref, gain_ref, out_ref):
    rows = x_ref.shape[0]
    meeting = cb_ref[...]
    c_rows = c_ref[...]
    low = first_half((rows, PAIR))
    low_row = jnp.where(first_half((1, PAIR)), 1.0, 0.0)
    keep_low = low_row.astype(BF16)
    keep_high = (1.0 - low_row).astype(BF16)
    for pair in range(x_ref.shape[1] // PAIR):
        cols = slice(pair * PAIR, (pair + 1) * PAIR)
        x_pair = x_ref[:, cols]
        mixers, fades = [], []
        for h in (2 * pair, 2 * pair + 1):
            run = run_ref[0, :, h : h + 1]
            spread = jnp.minimum(run - runt_ref[h : h + 1, :], 0.0)
            mixers.append((jnp.exp(spread) * meeting).astype(BF16))
            fades.append(jnp.exp(run))
        x_low, x_high = x_pair * keep_low, x_pair * keep_high
        if rows % 128 == 0:
            inside = jnp.dot(
                jnp.concatenate(mixers, axis=1),
                jnp.concatenate([x_low, x_high], axis=0),
                preferred_element_type=F32,
            )
        else:
            inside = jnp.dot(mixers[0], x_low, preferred_element_type=F32) + jnp.dot(
                mixers[1], x_high, preferred_element_type=F32
            )
        entering = jnp.dot(c_rows, state_ref[:, cols], preferred_element_type=F32)
        fade = jnp.where(low, fades[0], fades[1])
        out_ref[:, cols] = (
            inside + entering * fade + gain_ref[:, cols] * x_pair.astype(F32)
        ).astype(BF16)


def span_outputs(x, run, runt, meeting, c_rows, state, gain, block):
    rows, channels = x.shape
    heads = block // P_SIZE
    steps = channels // block
    run_blocks = run.reshape(rows, steps, heads).transpose(1, 0, 2)
    return pl.pallas_call(
        span_kernel,
        grid=(steps,),
        in_specs=[
            pl.BlockSpec((rows, block), lambda i: (0, i)),
            pl.BlockSpec((1, rows, heads), lambda i: (i, 0, 0)),
            pl.BlockSpec((heads, rows), lambda i: (i, 0)),
            pl.BlockSpec((rows, rows), lambda i: (0, 0)),
            pl.BlockSpec((rows, NS), lambda i: (0, 0)),
            pl.BlockSpec((NS, block), lambda i: (0, i)),
            pl.BlockSpec((1, block), lambda i: (0, i)),
        ],
        out_specs=pl.BlockSpec((rows, block), lambda i: (0, i)),
        out_shape=jax.ShapeDtypeStruct((rows, channels), BF16),
        compiler_params=pltpu.CompilerParams(vmem_limit_bytes=24 << 20),
        cost_estimate=pl.CostEstimate(
            flops=20 * rows * rows * channels,
            bytes_accessed=4 * rows * channels,
            transcendentals=rows * rows * channels // P_SIZE,
        ),
        name="span_outputs",
    )(x, run_blocks, runt, meeting, c_rows, state, gain)


def attention_kernel(
    heads, chunk, first, spread, place_ref, lo_ref, q_ref, kv_ref, *refs
):
    out_ref, kext, vext, top, accum = refs[-5:]
    step = pl.program_id(0)
    rows_here = q_ref.shape[0]
    layers, ctxs, piece = spread
    keys = kext.shape[0]

    @pl.when(step == 0)
    def _():
        vext[:, HD:] = jnp.ones((keys, HD), BF16)
        for z in range(layers):
            for c in range(ctxs):
                src = slice((z * ctxs + c) * piece, (z * ctxs + c + 1) * piece)
                dst = slice((c * layers + z) * piece, (c * layers + z + 1) * piece)
                kext[dst, :] = kv_ref[src, :HD]
                vext[dst, :HD] = kv_ref[src, HD:]

    pos = place_ref[first + step]
    lo_pos = lo_ref[first + step]
    last = pos // chunk
    lo_chunk = lo_pos // chunk
    scale = HD ** (-0.5) * LOG2E
    together = min(heads, 4)
    tall = together * rows_here

    def scores_of(part, start):
        q = jnp.concatenate(
            [q_ref[:, h * HD : (h + 1) * HD] for h in range(part * together, (part + 1) * together)],
            axis=0,
        )
        k = kext[pl.ds(start, chunk), :]
        return lax.dot_general(q, k, (((1,), (1,)), ((), ())), preferred_element_type=F32) * scale

    def gathered(terms, start):
        return jnp.dot(
            terms.astype(BF16), vext[pl.ds(start, chunk), :], preferred_element_type=F32
        )

    start = pl.multiple_of(last * chunk, chunk)
    key_pos = start + lax.broadcasted_iota(jnp.int32, (rows_here, chunk), 1)
    query_pos = pos + lax.broadcasted_iota(jnp.int32, (rows_here, chunk), 0)
    bias = jnp.where((key_pos <= query_pos) & (key_pos >= lo_pos), 0.0, NEG_FILL)
    bias = jnp.concatenate([bias] * together, axis=0)
    for part in range(heads // together):
        rows = slice(part * tall, (part + 1) * tall)
        scores = scores_of(part, start) + bias
        new_top = jnp.max(scores, axis=1, keepdims=True)
        top[rows, :] = jnp.broadcast_to(new_top, (tall, HD))
        accum[rows, :] = gathered(jnp.exp2(scores - new_top), start)

    def more(j, hide):
        start = pl.multiple_of(j * chunk, chunk)
        for part in range(heads // together):
            rows = slice(part * tall, (part + 1) * tall)
            scores = scores_of(part, start)
            if hide is not None:
                scores = scores + hide
            old_top = top[rows, :]
            new_top = jnp.maximum(old_top, jnp.max(scores, axis=1, keepdims=True))
            top[rows, :] = new_top
            fade = jnp.exp2(old_top - new_top)
            added = gathered(jnp.exp2(scores - new_top[:, :1]), start)
            accum[rows, :HD] = accum[rows, :HD] * fade + added[:, :HD]
            accum[rows, HD:] = accum[rows, HD:] * fade + added[:, HD:]

    @pl.when(lo_chunk < last)
    def _():
        key_pos = lo_chunk * chunk + lax.broadcasted_iota(jnp.int32, (1, chunk), 1)
        more(lo_chunk, jnp.where(key_pos >= lo_pos, 0.0, NEG_FILL))

    @pl.loop(lo_chunk + 1, last)
    def _(j):
        more(j, None)

    for head in range(heads):
        rows = slice(head * rows_here, (head + 1) * rows_here)
        out_ref[:, head * HD : (head + 1) * HD] = (
            accum[rows, :HD] / accum[rows, HD:]
        ).astype(BF16)


def attention(queries, kv, place, lo, rows, spread, first, count, earlier=None):
    total, width = queries.shape
    heads = width // HD
    keys = kv.shape[0]
    chunk = min(KEY_CHUNK, keys)
    in_specs = [
        pl.BlockSpec((rows, width), lambda i, *_: (i + first, 0)),
        pl.BlockSpec((keys, 2 * HD), lambda i, *_: (0, 0)),
    ]
    operands = [place, lo, queries, kv]
    aliases = {}
    if earlier is not None:
        in_specs.append(pl.BlockSpec(memory_space=pl.ANY))
        operands.append(earlier)
        aliases = {4: 0}
    return pl.pallas_call(
        functools.partial(attention_kernel, heads, chunk, first, spread),
        grid_spec=pltpu.PrefetchScalarGridSpec(
            num_scalar_prefetch=2,
            grid=(count,),
            in_specs=in_specs,
            out_specs=pl.BlockSpec((rows, width), lambda i, *_: (i + first, 0)),
            scratch_shapes=[
                pltpu.VMEM((keys, HD), BF16),
                pltpu.VMEM((keys, 2 * HD), BF16),
                pltpu.VMEM((heads * rows, HD), F32),
                pltpu.VMEM((heads * rows, 2 * HD), F32),
            ],
        ),
        out_shape=jax.ShapeDtypeStruct((total, width), BF16),
        input_output_aliases=aliases,
        compiler_params=pltpu.CompilerParams(vmem_limit_bytes=40 << 20),
        cost_estimate=pl.CostEstimate(
            flops=4 * count * rows * width * keys // 2,
            bytes_accessed=4 * count * rows * width + 2 * kv.size,
            transcendentals=count * rows * heads * keys // 2,
        ),
        name="attention",
    )(*operands)


def arrange_kernel(
    sizes, q_ref, k_ref, v_ref, d_ref, q_out, kv_out, d_out,
    own_sem, d_send, d_recv, k_send, k_recv, v_send, v_recv, q_send, q_recv,
    up_send, up_recv, down_send, down_recv,
):
    layers, ctxs, pairs, copies = sizes
    tp, members = layers * pairs, ctxs * pairs
    ctx, layer, pair = lax.axis_index("ctx"), lax.axis_index("tz"), lax.axis_index("ty")
    member, place = ctx * pairs + pair, layer * pairs + pair
    width = q_out.shape[2]

    def in_plane(j):
        return {"ctx": j // pairs, "ty": j % pairs}

    def in_tp(j):
        return {"tz": j // pairs, "ty": j % pairs}

    def send(src, dst, send_sem, recv_sem, device):
        return pltpu.make_async_remote_copy(
            src_ref=src,
            dst_ref=dst,
            send_sem=send_sem,
            recv_sem=recv_sem,
            device_id=device,
            device_id_type=pl.DeviceIdType.MESH,
        )

    def columns(j, size):
        return pl.ds(pl.multiple_of(j * size, size), size)

    barrier = pltpu.get_barrier_semaphore()
    for d in range(1, members):
        pl.semaphore_signal(
            barrier, inc=1, device_id=in_plane((member + d) % members),
            device_id_type=pl.DeviceIdType.MESH,
        )
    for d in range(1, tp):
        pl.semaphore_signal(
            barrier, inc=1, device_id=in_tp((place + d) % tp),
            device_id_type=pl.DeviceIdType.MESH,
        )
    pl.semaphore_wait(barrier, members - 1 + tp - 1)

    first, decays, later = [], [], []
    for d in range(1, members):
        j = (member + d) % members
        cols = columns(j // copies, HD)
        for src, half, s_sem, r_sem in (
            (k_ref, 0, k_send, k_recv),
            (v_ref, 1, v_send, v_recv),
        ):
            first.append(
                send(
                    src.at[:, cols],
                    kv_out.at[layer, member, :, half * HD : (half + 1) * HD],
                    s_sem.at[d - 1],
                    r_sem.at[d - 1],
                    in_plane(j),
                )
            )
    for copy in first:
        copy.start()
    for d in range(1, tp):
        j = (place + d) % tp
        decays.append(
            send(d_ref.at[j], d_out.at[place], d_send.at[d - 1], d_recv.at[d - 1], in_tp(j))
        )
    for copy in decays:
        copy.start()
    own_cols = columns(member // copies, HD)
    own_kv = [
        pltpu.make_async_copy(
            k_ref.at[:, own_cols], kv_out.at[layer, member, :, :HD], own_sem.at[0]
        ),
        pltpu.make_async_copy(
            v_ref.at[:, own_cols], kv_out.at[layer, member, :, HD:], own_sem.at[1]
        ),
    ]
    own_rest = [
        pltpu.make_async_copy(q_ref.at[:, columns(member, width)], q_out.at[member], own_sem.at[2]),
        pltpu.make_async_copy(d_ref.at[place], d_out.at[place], own_sem.at[3]),
    ]
    for copy in own_kv + own_rest:
        copy.start()
    for copy in own_kv:
        copy.wait()
    for copy in first:
        copy.wait_recv()

    def up(step, piece):
        block = kv_out.at[layer - step, piece * pairs : (piece + 1) * pairs]
        return send(
            block, block, up_send.at[step, piece], up_recv.at[step, piece], {"tz": layer + 1}
        )

    def down(step, piece):
        block = kv_out.at[layer + step, piece * pairs : (piece + 1) * pairs]
        return send(
            block, block, down_send.at[step, piece], down_recv.at[step, piece], {"tz": layer - 1}
        )

    for step in range(layers):
        for piece in range(ctxs):
            if step > 0:

                @pl.when(layer - step >= 0)
                def _():
                    up(step - 1, piece).wait_recv()

            if step < layers - 1:

                @pl.when((layer - step >= 0) & (layer < layers - 1))
                def _():
                    up(step, piece).start()

            if step > 0:

                @pl.when(layer + step <= layers - 1)
                def _():
                    down(step - 1, piece).wait_recv()

            if step < layers - 1:

                @pl.when((layer + step <= layers - 1) & (layer > 0))
                def _():
                    down(step, piece).start()

        if step == 0:
            for d in range(1, members):
                j = (member + d) % members
                later.append(
                    send(
                        q_ref.at[:, columns(j, width)],
                        q_out.at[member],
                        q_send.at[d - 1],
                        q_recv.at[d - 1],
                        in_plane(j),
                    )
                )
            for copy in later:
                copy.start()

    for step in range(layers - 1):
        for piece in range(ctxs):

            @pl.when((layer - step >= 0) & (layer < layers - 1))
            def _():
                up(step, piece).wait_send()

            @pl.when((layer + step <= layers - 1) & (layer > 0))
            def _():
                down(step, piece).wait_send()

    for copy in first:
        copy.wait_send()
    for copy in decays + later:
        copy.wait()
    for copy in own_rest:
        copy.wait()


def arrange(queries, keys, values, decays, sizes):
    layers, ctxs, pairs, _ = sizes
    tp, members = layers * pairs, ctxs * pairs
    rows = queries.shape[0]
    width = queries.shape[1] // members
    anywhere = pl.BlockSpec(memory_space=pl.ANY)
    dma = pltpu.SemaphoreType.DMA
    return pl.pallas_call(
        functools.partial(arrange_kernel, sizes),
        in_specs=[anywhere] * 4,
        out_specs=[anywhere] * 3,
        out_shape=[
            jax.ShapeDtypeStruct((members, rows, width), BF16),
            jax.ShapeDtypeStruct((layers, members, rows, 2 * HD), BF16),
            jax.ShapeDtypeStruct(decays.shape, F32),
        ],
        scratch_shapes=[dma((4,))]
        + [dma((tp - 1,))] * 2
        + [dma((members - 1,))] * 6
        + [dma((layers - 1, ctxs))] * 4,
        compiler_params=pltpu.CompilerParams(collective_id=0, has_side_effects=True),
        cost_estimate=pl.CostEstimate(
            flops=0, bytes_accessed=4 * queries.size, transcendentals=0
        ),
        name="arrange",
    )(queries, keys, values, decays)


def per_device(
    mamba_in, state_in_b, state_out_c, step_decay, skip_gain, queries, keys, values, doc_ids
):
    tp_axes, plane, everyone = ("tz", "ty"), ("ctx", "ty"), ("ctx", "tz", "ty")
    layers, pairs, ctxs = lax.axis_size("tz"), lax.axis_size("ty"), lax.axis_size("ctx")
    tp, members = layers * pairs, ctxs * pairs
    layer = lax.axis_index("tz")
    tp_rank = layer * pairs + lax.axis_index("ty")
    rows, channels = mamba_in.shape
    groups = step_decay.shape[1]

    by_owner = step_decay.reshape(tp, rows, groups).transpose(0, 2, 1)
    gain_rows = jnp.pad(skip_gain[None, :], ((0, 7), (0, rows - groups)))
    sent = jnp.concatenate([by_owner, jnp.broadcast_to(gain_rows, (tp, 8, rows))], axis=1)

    query_cols, kv, got = arrange(
        queries, keys, values, sent, (layers, ctxs, pairs, members // KVH)
    )
    query_cols = query_cols.reshape(members * rows, queries.shape[1] // members)
    kv = kv.reshape(layers * members * rows, 2 * HD)
    decay_t = got[:, :groups, :].reshape(tp * groups, rows)
    gains = got[:, groups, :groups].reshape(tp * groups)

    b_rows = lax.dynamic_slice_in_dim(state_in_b, tp_rank * rows, rows, 0)
    c_rows = lax.dynamic_slice_in_dim(state_out_c, tp_rank * rows, rows, 0)
    lower = jnp.tril(jnp.ones((rows, rows), F32))
    run_t = jnp.dot(decay_t, lower.T, precision=HIGHEST)
    run = run_t.T
    driven_run_t = run_t - 0.5 * jnp.log(-jnp.expm1(2.0 * decay_t))
    total = run_t[:, -1:]
    remain_t = jnp.exp(jnp.minimum(total - driven_run_t, 0.0))
    meeting = jnp.dot(c_rows, b_rows.T, precision=HIGHEST) * lower
    ends = end_states(mamba_in, remain_t, b_rows.T, 2048)
    total_row = jnp.repeat(total[:, 0], P_SIZE)[None, :]
    totals = lax.all_to_all(total_row, everyone, split_axis=1, concat_axis=0, tiled=True)

    member = jnp.arange(members, dtype=jnp.int32)
    place = ((member // pairs) * tp + layer * pairs + member % pairs) * rows
    docs_here = doc_ids[place // BLK]
    lo = BLK * jnp.sum(doc_ids[None, :] < docs_here[:, None], axis=1).astype(jnp.int32)
    spread = (layers, ctxs, pairs * rows)
    half = members // 2

    parts = lax.all_to_all(ends, everyone, split_axis=1, concat_axis=0, tiled=True)
    attn_first = attention(query_cols, kv, place, lo, rows, spread, 0, half)
    parts, attn_first = lax.optimization_barrier((parts, attn_first))
    before = prefix_states(parts, totals)
    before, attn_first = lax.optimization_barrier((before, attn_first))
    state = lax.all_to_all(before, everyone, split_axis=0, concat_axis=1, tiled=True)
    attn_rows = attention(
        query_cols, kv, place, lo, rows, spread, half, members - half, attn_first
    )
    attn_rows, state = lax.optimization_barrier((attn_rows, state))
    attn_out = lax.all_to_all(attn_rows, plane, split_axis=0, concat_axis=1, tiled=True)
    mamba_out = span_outputs(
        mamba_in,
        run,
        driven_run_t,
        meeting,
        c_rows.astype(BF16),
        state,
        jnp.repeat(gains, P_SIZE)[None, :],
        1024,
    )
    return (mamba_out, attn_out)


def solution(mesh):
    ctxs, tp = mesh.devices.shape
    split = jax.sharding.Mesh(mesh.devices.reshape(ctxs, tp // 2, 2), ("ctx", "tz", "ty"))
    tokens = P(("ctx", "tz", "ty"), None)
    in_specs = (
        tokens,
        P("ctx", None),
        P("ctx", None),
        P("ctx", ("tz", "ty")),
        P(("tz", "ty")),
        tokens,
        tokens,
        tokens,
        P(),
    )
    return jax.shard_map(
        per_device, mesh=split, in_specs=in_specs, out_specs=(tokens, tokens), check_vma=False
    )
```
